32 devices in a mesh: span: 8 (over z, core), wall: 4 (over y, x).
Axes of the slice: x: 2, y: 2, z: 4, core: 2. Of those that a mesh axis runs over, the one named last changes fastest.
Arguments:
- field: float32 [5, 5, 5, 8, 8, 128], P(None, None, None, 'span', 'wall'), may hold values from -6 to 6
- velocity: float32 [3, 5, 5, 5, 8, 8, 128], P(None, None, None, None, 'span', 'wall'), may hold values from -6 to 6
- cells: int32 [4096], P(('span', 'wall')), may hold values from 0 to 255
- destination: int32 [4096, 1], P(('span', 'wall')), may hold values from 0 to 7; in each aligned block of 128 rows (0 to 127, 128 to 255, ...) at most 16 rows name the same one
- targets: bfloat16 [4096, 128], P(('span', 'wall')), may hold values from -6 to 6
- weight_in: bfloat16 [8, 128, 256], P('span'), may hold values from -0.5 to 0.5
- weight_two: bfloat16 [8, 256, 256], P('span'), may hold values from -0.375 to 0.375
- weight_three: bfloat16 [8, 256, 256], P('span'), may hold values from -0.375 to 0.375
- weight_four: bfloat16 [8, 256, 256], P('span'), may hold values from -0.375 to 0.375
- weight_out: bfloat16 [8, 256, 128], P('span'), may hold values from -0.375 to 0.375
Outputs:
- new_field: float32 [5, 5, 5, 8, 8, 128], P(None, None, None, 'span', 'wall')
- grad_in: float32 [8, 128, 256], P('span')
- grad_two: float32 [8, 256, 256], P('span')
- grad_three: float32 [8, 256, 256], P('span')
- grad_four: float32 [8, 256, 256], P('span')
- grad_out: float32 [8, 256, 128], P('span')
The draws below stay inside these ranges and needn't reach their ends.
Inputs may be any that keep to these rules, and one draw needn't show every extreme that they name: `cells`: A local element index of the owning device. `destination`: among the 128 rows of one device at most 16 name the same station, and in every draw some device has exactly 16 rows naming one station.
All inputs are finite; a program needn't handle non-finite values.
Results may differ from the reference program's by a relative error of at most 0.0065.
Values may be sent and summed in bfloat16 or wider, within the bound.
A program may use at most 64 MiB of HBM per device.

```python
import math
import jax
import jax.numpy as jnp
import numpy as np
from jax import lax

P_SIZE = 5
EA = 1
EB = 2
EC = 128
S = 128
HID = 256
OUT = 128
CAP = 16
FEAT = 128
NA = 8
NB = 8
ROWS = 4096
N_SPAN = 8
N_WALL = 4


def set_ends(entries, own_key, least, top_value):
    spot = [jax.random.randint(jax.random.fold_in(own_key, axis), (), 0, length) for axis, length in enumerate(entries.shape)]
    widest = entries.shape.index(max(entries.shape))
    neighbour = spot[:widest] + [(spot[widest] + 1) % entries.shape[widest]] + spot[widest + 1:]
    return entries.at[tuple(spot)].set(least).at[tuple(neighbour)].set(top_value)


def levels(own_key, extent, cuts, least, high):
    gain = 1.0
    for axis_at, parts in cuts:
        steps = jax.random.uniform(jax.random.fold_in(jax.random.fold_in(own_key, 6), axis_at), (parts,), jnp.float32, least / len(cuts), high / len(cuts))
        gain = gain * jnp.repeat(jnp.exp(steps), extent[axis_at] // parts).reshape((-1,) + (1,) * (len(extent) - 1 - axis_at))
    return gain


def assign_block(key, own, number, rows, count, top, reach, lean):
    ranking = jax.random.permutation(key, count)
    packed, common = load_shares(count, rows * top, reach, lean, True), load_shares(count, rows * top, reach, lean, False)
    places = jnp.arange(count)

    def named(sizes, turn):
        used = int((sizes > 0).sum())
        fixed = max(1, used // 4)
        passed = fixed + (places - fixed + turn * (used - fixed)) % max(1, count - fixed)
        return jnp.zeros((count,), jnp.int32).at[ranking[jnp.where(places < fixed, places, passed)]].set(jnp.asarray(sizes, jnp.int32))

    sizes = jnp.where(number % 4 == 0, named(packed, number // 4), named(common, number - number // 4 - 1))
    mixed = jax.random.permutation(jax.random.fold_in(own, 3), count)
    giver, taker = mixed[0:count // 2 * 2:2], mixed[1:count // 2 * 2:2]
    margin = jnp.minimum(sizes[giver] - 1, reach - sizes[taker]) // 2
    margin = jnp.where((giver == ranking[0]) | (taker == ranking[0]) | (sizes[taker] == 0), 0, jnp.maximum(margin, 0))
    passed = jax.random.randint(jax.random.fold_in(own, 4), (count // 2,), 0, 1 << 20) % (margin + 1)
    sizes = sizes.at[giver].add(-passed).at[taker].add(passed)
    members = jnp.searchsorted(jnp.cumsum(sizes), jnp.arange(rows * top), side="right").astype(jnp.int32)
    grid = members.reshape(top, rows).T
    grid = grid[jax.random.permutation(jax.random.fold_in(own, 1), rows)]
    turn = jax.random.randint(jax.random.fold_in(own, 2), (rows, 1), 0, top)
    return jnp.take_along_axis(grid, (jnp.arange(top)[None, :] + turn) % top, axis=1)


def load_shares(number_of, total, reach, skew, full):
    portions = [(1 << 20) // math.isqrt(grade ** skew) + 1 for grade in range(1, number_of + 1)]
    largest = reach if full else min(reach, max(-(-total // number_of), total * portions[0] // sum(portions)))
    least = 1 if total - largest >= number_of - 1 else 0
    holding, spare = [largest] + [least] * (number_of - 1), total - largest - least * (number_of - 1)
    while spare > 0:
        free = [i for i in range(1, number_of) if holding[i] < largest] or [i for i in range(1, number_of) if holding[i] < reach]
        whole, left = sum([portions[i] for i in free]), spare
        for i in free:
            extra = min(reach - holding[i], max(1, left * portions[i] // whole), spare)
            holding[i] = holding[i] + extra
            spare = spare - extra
    return np.array(holding)


def centred(own_key, shape, scale, reach, shards=(), kind=jnp.bfloat16):
    level = levels(own_key, shape, shards, -0.22, 0.18) if shards else 1.0
    result = jax.random.normal(own_key, shape, jnp.float32) * scale * level
    return jnp.minimum(jnp.maximum(result, -reach), reach).astype(kind)


def setup_inputs(seed: int = 0) -> dict:
    key_list = jax.random.split(jax.random.key(seed), 11)
    field = centred(key_list[0], (P_SIZE, P_SIZE, P_SIZE, NA, NB, EC), 1.0, 6.0, ((3, 8), (4, 4)), jnp.float32)
    velocity = centred(key_list[1], (3, P_SIZE, P_SIZE, P_SIZE, NA, NB, EC), 1.0, 6.0, ((4, 8), (5, 4)), jnp.float32)
    cells = set_ends(jax.random.randint(key_list[2], (ROWS,), 0, EA * EB * EC), jax.random.fold_in(key_list[2], 1), 0, (EA * EB * EC) - 1).astype(jnp.int32)
    destination_keys = jax.random.split(jax.random.fold_in(key_list[3], 1), ROWS // S)
    destination_turns = jax.random.permutation(jax.random.fold_in(key_list[3], 3), ROWS // S)
    destination = jax.vmap(lambda own, number: assign_block(jax.random.fold_in(key_list[3], 2), own, number, S, N_SPAN, 1, CAP, 2))(destination_keys, destination_turns).reshape((ROWS, 1))
    targets = centred(key_list[4], (ROWS, OUT), 1.0, 6.0, ((0, 32),))
    weight_in = centred(key_list[5], (N_SPAN, FEAT, HID), FEAT ** -0.5, 0.5, ((0, 8),))
    weight_two = centred(key_list[6], (N_SPAN, HID, HID), HID ** -0.5, 0.375, ((0, 8),))
    weight_three = centred(key_list[7], (N_SPAN, HID, HID), HID ** -0.5, 0.375, ((0, 8),))
    weight_four = centred(key_list[8], (N_SPAN, HID, HID), HID ** -0.5, 0.375, ((0, 8),))
    weight_out = centred(key_list[9], (N_SPAN, HID, OUT), HID ** -0.5, 0.375, ((0, 8),))
    return dict(field=field, velocity=velocity, cells=cells, destination=destination, targets=targets, weight_in=weight_in, weight_two=weight_two, weight_three=weight_three, weight_four=weight_four, weight_out=weight_out)


step_scale = 0.04

def legendre_pair(order, point):
    value_prev = 1.0
    value_now = point
    slope_prev = 0.0
    slope_now = 1.0
    if order == 0:
        return (1.0, 0.0)
    for degree in range(1, order):
        value_next = ((2 * degree + 1) * point * value_now - degree * value_prev) / (degree + 1)
        slope_next = slope_prev + (2 * degree + 1) * value_now
        value_prev, value_now = (value_now, value_next)
        slope_prev, slope_now = (slope_now, slope_next)
    return (value_now, slope_now)

def gauss_nodes(count):
    found = []
    for index in range(count):
        guess = math.cos(math.pi * (index + 0.75) / (count + 0.5))
        for sweep in range(60):
            value, slope = legendre_pair(count, guess)
            guess = guess - value / slope
        found.append(guess)
    return sorted(found)

def fr_tables():
    nodes = gauss_nodes(P_SIZE)
    bary = []
    for j in range(P_SIZE):
        product = 1.0
        for m in range(P_SIZE):
            if m != j:
                product = product * (nodes[j] - nodes[m])
        bary.append(1.0 / product)
    deriv = [[0.0] * P_SIZE for row_index in range(P_SIZE)]
    for i in range(P_SIZE):
        for j in range(P_SIZE):
            if i != j:
                deriv[i][j] = bary[j] / bary[i] / (nodes[i] - nodes[j])
        deriv[i][i] = -sum((deriv[i][j] for j in range(P_SIZE) if j != i))

    def basis_at(point):
        values = []
        for j in range(P_SIZE):
            product = 1.0
            for m in range(P_SIZE):
                if m != j:
                    product = product * (point - nodes[m]) / (nodes[j] - nodes[m])
            values.append(product)
        return values
    left_value = basis_at(-1.0)
    right_value = basis_at(1.0)
    sign = (-1.0) ** P_SIZE
    slope_left = [0.5 * sign * (legendre_pair(P_SIZE, x)[1] - legendre_pair(P_SIZE - 1, x)[1]) for x in nodes]
    slope_right = [-slope_left[P_SIZE - 1 - i] for i in range(P_SIZE)]
    return tuple((jnp.asarray(table, jnp.float32) for table in (deriv, left_value, right_value, slope_left, slope_right)))

def along(matrix, field, axis):
    return jnp.moveaxis(jnp.tensordot(matrix, field, axes=([1], [axis]), precision=lax.Precision.HIGHEST), 0, axis)

def at_face(vector, field, axis):
    return jnp.tensordot(vector, field, axes=([0], [axis]), precision=lax.Precision.HIGHEST)

def spread(face, vector, axis, ndim):
    target_shape = [1] * ndim
    target_shape[axis] = vector.shape[0]
    return jnp.expand_dims(face, axis) * vector.reshape(target_shape)

def upwind(state_before, speed_before, state_after, speed_after):
    mean_speed = 0.5 * (speed_before + speed_after)
    return 0.5 * mean_speed * (state_before + state_after) - 0.5 * jnp.abs(mean_speed) * (state_after - state_before)

def face_states(field, speed, axis, tables):
    left_value = tables[1]
    right_value = tables[2]
    return (at_face(left_value, field, axis), at_face(left_value, speed, axis), at_face(right_value, field, axis), at_face(right_value, speed, axis))

def divergence(field, speed, axis, own, before, after, tables):
    deriv, left_value, right_value, slope_left, slope_right = tables
    flux = speed * field
    volume = along(deriv, flux, axis)
    flux_left = at_face(left_value, flux, axis)
    flux_right = at_face(right_value, flux, axis)
    common_left = upwind(before[0], before[1], own[0], own[1])
    common_right = upwind(own[2], own[3], after[0], after[1])
    return volume + spread(common_left - flux_left, slope_left, axis, field.ndim) + spread(common_right - flux_right, slope_right, axis, field.ndim)

def forward(inputs, weights):
    acts = [inputs]
    pres = []
    hidden = inputs
    for layer in weights[:-1]:
        pre = jnp.dot(hidden, layer, preferred_element_type=jnp.float32)
        pres.append(pre)
        hidden = jax.nn.silu(pre).astype(jnp.bfloat16)
        acts.append(hidden)
    return (jnp.dot(hidden, weights[-1], preferred_element_type=jnp.float32), acts, pres)

def backward_layer(error, weight, pre):
    back = lax.dot_general(error, weight, (((1,), (1,)), ((), ())), preferred_element_type=jnp.float32)
    sigma = jax.nn.sigmoid(pre)
    return (back * sigma * (1.0 + pre * (1.0 - sigma))).astype(jnp.bfloat16)

def weight_grad(act, error):
    return lax.dot_general(act, error, (((0,), (0,)), ((), ())), preferred_element_type=jnp.float32)

def row_grads(inputs, targets, row_scale, weights):
    output, acts, pres = forward(inputs, weights)
    error = (row_scale[:, None] * (output - targets.astype(jnp.float32))).astype(jnp.bfloat16)
    grads = [None] * 5
    grads[4] = weight_grad(acts[4], error)
    for layer_index in range(3, -1, -1):
        error = backward_layer(error, weights[layer_index + 1], pres[layer_index])
        grads[layer_index] = weight_grad(acts[layer_index], error)
    return tuple(grads)

def shift_down(face, axis):
    widths = [(1, 0) if dim_index == axis else (0, 0) for dim_index in range(face.ndim)]
    return lax.slice_in_dim(jnp.pad(face, widths), 0, face.shape[axis], axis=axis)

def shift_up(face, axis):
    widths = [(0, 1) if dim_index == axis else (0, 0) for dim_index in range(face.ndim)]
    return lax.slice_in_dim(jnp.pad(face, widths), 1, face.shape[axis] + 1, axis=axis)

def reference(field, velocity, cells, destination, targets, weight_in, weight_two, weight_three, weight_four, weight_out):
    tables = fr_tables()
    total = jnp.zeros_like(field)
    for direction in range(3):
        speed = velocity[direction]
        own = face_states(field, speed, direction, tables)
        face_axis = 2 + direction
        if direction < 2:
            before = (shift_down(own[2], face_axis), shift_down(own[3], face_axis))
            after = (shift_up(own[0], face_axis), shift_up(own[1], face_axis))
        else:
            before = (jnp.roll(own[2], 1, face_axis), jnp.roll(own[3], 1, face_axis))
            after = (jnp.roll(own[0], -1, face_axis), jnp.roll(own[1], -1, face_axis))
        total = total + divergence(field, speed, direction, own, before, after, tables)
    new_field = field - step_scale * total
    devices_all = N_SPAN * N_WALL
    local_count = EA * EB * EC
    point_values = new_field.reshape(P_SIZE * P_SIZE * P_SIZE, N_SPAN, EA, N_WALL, EB, EC)
    point_values = point_values.transpose(1, 3, 0, 2, 4, 5).reshape(devices_all, P_SIZE * P_SIZE * P_SIZE, local_count)
    speed_means = lax.optimization_barrier(jnp.mean(velocity.reshape(3, P_SIZE * P_SIZE * P_SIZE, N_SPAN, EA, N_WALL, EB, EC), axis=1))
    speed_means = speed_means.transpose(1, 3, 0, 2, 4, 5).reshape(devices_all, 3, local_count)
    values = jnp.concatenate([point_values, speed_means], axis=1)
    picked = jnp.take_along_axis(values, cells.reshape(devices_all, 1, S).astype(jnp.int32), axis=2)
    rows = picked.transpose(0, 2, 1).reshape(ROWS, FEAT).astype(jnp.bfloat16)
    dest = destination[:, 0].astype(jnp.int32)
    wall_index = jnp.arange(ROWS, dtype=jnp.int32) // S % N_WALL
    shard = dest * N_WALL + wall_index
    counts = jax.ops.segment_sum(jnp.ones((ROWS,), jnp.float32), shard, num_segments=devices_all)
    row_scale = 1.0 / counts[shard]
    onehot = (dest.reshape(devices_all, S, 1) == jnp.arange(N_SPAN, dtype=jnp.int32)[None, None, :]).astype(jnp.int32)
    slots = lax.optimization_barrier(jnp.sum((jnp.cumsum(onehot, axis=1) - 1) * onehot, axis=2)).reshape(ROWS).astype(jnp.int32)
    place = jnp.arange(ROWS, dtype=jnp.int32) // S * CAP + slots
    slot_total = devices_all * CAP
    targets_f = targets

    def station(carry, xs):
        station_weights = xs[:5]
        station_index = xs[5]
        where_to = jnp.where(dest == station_index, place, slot_total).astype(jnp.int32)
        in_rows = jnp.zeros((slot_total, FEAT), jnp.bfloat16).at[where_to].set(rows, mode='drop')
        in_targets = jnp.zeros((slot_total, OUT), jnp.bfloat16).at[where_to].set(targets_f, mode='drop')
        in_scale = jnp.zeros((slot_total,), jnp.float32).at[where_to].set(row_scale, mode='drop')
        grads = row_grads(in_rows, in_targets, in_scale, station_weights)
        return (carry, grads)
    xs = (weight_in, weight_two, weight_three, weight_four, weight_out, jnp.arange(N_SPAN, dtype=jnp.int32))
    unused_carry, grads = lax.scan(station, jnp.zeros((), jnp.int32), xs)
    return (new_field, grads[0], grads[1], grads[2], grads[3], grads[4])
```

```python
import functools
import math

import jax
import jax.numpy as jnp
import numpy as np
from jax import lax
from jax.experimental import pallas as pl
from jax.experimental.pallas import tpu as pltpu
from jax.sharding import PartitionSpec as P

P_SIZE = 5
CAP = 16
MESH = pl.DeviceIdType.MESH


step_scale = 0.04


def legendre_pair(order, point):
    value_prev = 1.0
    value_now = point
    slope_prev = 0.0
    slope_now = 1.0
    for degree in range(1, order):
        value_next = ((2 * degree + 1) * point * value_now - degree * value_prev) / (degree + 1)
        slope_next = slope_prev + (2 * degree + 1) * value_now
        value_prev, value_now = (value_now, value_next)
        slope_prev, slope_now = (slope_now, slope_next)
    return (value_now, slope_now)


def gauss_nodes(count):
    found = []
    for index in range(count):
        guess = math.cos(math.pi * (index + 0.75) / (count + 0.5))
        for sweep in range(60):
            value, slope = legendre_pair(count, guess)
            guess = guess - value / slope
        found.append(guess)
    return sorted(found)


def fr_tables():
    nodes = gauss_nodes(P_SIZE)
    bary = []
    for j in range(P_SIZE):
        product = 1.0
        for m in range(P_SIZE):
            if m != j:
                product = product * (nodes[j] - nodes[m])
        bary.append(1.0 / product)
    deriv = [[0.0] * P_SIZE for row_index in range(P_SIZE)]
    for i in range(P_SIZE):
        for j in range(P_SIZE):
            if i != j:
                deriv[i][j] = bary[j] / bary[i] / (nodes[i] - nodes[j])
        deriv[i][i] = -sum((deriv[i][j] for j in range(P_SIZE) if j != i))

    def basis_at(point):
        values = []
        for j in range(P_SIZE):
            product = 1.0
            for m in range(P_SIZE):
                if m != j:
                    product = product * (point - nodes[m]) / (nodes[j] - nodes[m])
            values.append(product)
        return values

    left_value = basis_at(-1.0)
    right_value = basis_at(1.0)
    sign = (-1.0) ** P_SIZE
    slope_left = [
        0.5 * sign * (legendre_pair(P_SIZE, x)[1] - legendre_pair(P_SIZE - 1, x)[1]) for x in nodes
    ]
    slope_right = [-slope_left[P_SIZE - 1 - i] for i in range(P_SIZE)]
    inner = [
        [
            step_scale
            * (deriv[i][m] - slope_left[i] * left_value[m] - slope_right[i] * right_value[m])
            for m in range(P_SIZE)
        ]
        for i in range(P_SIZE)
    ]
    edge_left = [0.25 * step_scale * s for s in slope_left]
    edge_right = [0.25 * step_scale * s for s in slope_right]
    return inner, left_value, right_value, edge_left, edge_right


INNER, LEFT, RIGHT, EDGE_LEFT, EDGE_RIGHT = fr_tables()
RANGE = range(P_SIZE)


def weighted(table, parts):
    total = parts[0] * np.float32(table[0])
    for weight, part in zip(table[1:], parts[1:]):
        total = total + part * np.float32(weight)
    return total


def upwind(state_before, speed_before, state_after, speed_after):
    speed = speed_before + speed_after
    return speed * (state_before + state_after) - jnp.abs(speed) * (state_after - state_before)


def swap(x):
    return jnp.concatenate([x[..., 1:2, :], x[..., 0:1, :]], axis=-2)


def shift(x, step):
    return jnp.concatenate([x[..., -step:], x[..., :-step]], axis=-1)


def section_kernel(
    spans, walls,
    field_hbm, velocity_hbm, cells_ref, dest_ref, targets_ref,
    new_ref, rows_all, marks_all,
    field, velocity, own_zero, own_one, zero_before, zero_after, one_before, one_after,
    flat, rows_send, marks_send,
    in_sems, halo_send, halo_recv,
    marks_a_send, marks_a_recv, marks_b_send, marks_b_recv,
    rows_a_send, rows_a_recv, rows_b_send, rows_b_recv,
):
    i = lax.axis_index("span")
    w = lax.axis_index("wall")
    loads = [pltpu.make_async_copy(field_hbm, field, in_sems.at[0])]
    for d in range(3):
        loads.append(pltpu.make_async_copy(velocity_hbm.at[d], velocity.at[d], in_sems.at[1 + d]))
    for load in loads:
        load.start()

    barrier = pltpu.get_barrier_semaphore()
    for d in range(1, spans):
        pl.semaphore_signal(barrier, inc=1, device_id={"span": lax.rem(i + d, spans)}, device_id_type=MESH)
    for d in range(1, walls):
        pl.semaphore_signal(barrier, inc=1, device_id={"wall": lax.rem(w + d, walls)}, device_id_type=MESH)

    for at_end, ref in ((i == 0, zero_before), (i == spans - 1, zero_after), (w == 0, one_before), (w == walls - 1, one_after)):
        @pl.when(at_end)
        def _(ref=ref):
            ref[...] = jnp.zeros_like(ref)

    loads[0].wait()
    loads[1].wait()
    for j in RANGE:
        q = [field[m, j] for m in RANGE]
        a = [velocity[0, m, j] for m in RANGE]
        own_zero[0, j] = weighted(LEFT, q)
        own_zero[1, j] = weighted(LEFT, a)
        own_zero[2, j] = weighted(RIGHT, q)
        own_zero[3, j] = weighted(RIGHT, a)
    loads[2].wait()
    for m0 in RANGE:
        q = [field[m0, m] for m in RANGE]
        a = [velocity[1, m0, m] for m in RANGE]
        own_one[0, m0] = weighted(LEFT, q)
        own_one[1, m0] = weighted(LEFT, a)
        own_one[2, m0] = weighted(RIGHT, q)
        own_one[3, m0] = weighted(RIGHT, a)

    pl.semaphore_wait(barrier, spans + walls - 2)

    def halo(number, axis, place, count, own, into, right):
        peer = jnp.minimum(place + 1, count - 1) if right else jnp.maximum(place - 1, 0)
        copy = pltpu.make_async_remote_copy(
            src_ref=own.at[pl.ds(2 if right else 0, 2)],
            dst_ref=into,
            send_sem=halo_send.at[number],
            recv_sem=halo_recv.at[number],
            device_id={axis: peer},
            device_id_type=MESH,
        )
        sends = place < count - 1 if right else place > 0
        gets = place > 0 if right else place < count - 1
        return copy, sends, gets

    halos = [
        halo(0, "span", i, spans, own_zero, zero_before, True),
        halo(1, "span", i, spans, own_zero, zero_after, False),
        halo(2, "wall", w, walls, own_one, one_before, True),
        halo(3, "wall", w, walls, own_one, one_after, False),
    ]
    for copy, sends, _ in halos:
        pl.when(sends)(copy.start)

    samples = dest_ref.shape[1]
    dest = dest_ref[...]
    across = jnp.broadcast_to(dest, (samples, samples))
    down = jnp.transpose(across)
    earlier = lax.broadcasted_iota(jnp.int32, (samples, samples), 0) < lax.broadcasted_iota(jnp.int32, (samples, samples), 1)
    slot = jnp.sum(jnp.where(jnp.logical_and(across == down, earlier), 1.0, 0.0), axis=0, keepdims=True)
    position = dest * CAP + slot.astype(jnp.int32)
    places = spans * CAP
    chosen = jnp.where(
        lax.broadcasted_iota(jnp.int32, (places, samples), 0) == position, 1.0, 0.0
    ).astype(jnp.bfloat16)
    wanted = jnp.dot(chosen, targets_ref[...], preferred_element_type=jnp.float32)
    flags = jnp.dot(chosen, jnp.ones((samples, samples), jnp.bfloat16), preferred_element_type=jnp.float32)
    marks_send[:, 0:CAP] = wanted.astype(jnp.bfloat16).reshape(spans, CAP, -1)
    marks_send[:, CAP : 2 * CAP] = flags.astype(jnp.bfloat16).reshape(spans, CAP, -1)

    def dispatch(send, held, send_sems, recv_sems):
        copies = []
        for d in range(1, spans):
            peer = lax.rem(i + d, spans)
            copies.append(
                pltpu.make_async_remote_copy(
                    src_ref=send.at[peer],
                    dst_ref=held.at[w, i],
                    send_sem=send_sems.at[d],
                    recv_sem=recv_sems.at[d],
                    device_id={"span": peer},
                    device_id_type=MESH,
                )
            )
        for copy in copies:
            copy.start()
        held[w, i] = send[i]
        return copies

    def arrive(held, copies, recv_sems, send_sems):
        for d in range(1, spans):
            source = lax.rem(i + spans - d, spans)
            pltpu.make_async_remote_copy(
                src_ref=held.at[w, source],
                dst_ref=held.at[w, source],
                send_sem=send_sems.at[d],
                recv_sem=recv_sems.at[d],
                device_id={"span": source},
                device_id_type=MESH,
            ).wait_recv()

    def gather(held, send_sems, recv_sems):
        copies = []
        for d in range(1, walls):
            copies.append(
                pltpu.make_async_remote_copy(
                    src_ref=held.at[w],
                    dst_ref=held.at[w],
                    send_sem=send_sems.at[d],
                    recv_sem=recv_sems.at[d],
                    device_id={"wall": lax.rem(w + d, walls)},
                    device_id_type=MESH,
                )
            )
        for copy in copies:
            copy.start()
        return copies

    def gathered(held, copies, send_sems, recv_sems):
        for d in range(1, walls):
            source = lax.rem(w + walls - d, walls)
            pltpu.make_async_remote_copy(
                src_ref=held.at[source],
                dst_ref=held.at[source],
                send_sem=send_sems.at[d],
                recv_sem=recv_sems.at[d],
                device_id={"wall": source},
                device_id_type=MESH,
            ).wait_recv()
        for copy in copies:
            copy.wait_send()

    marks_a = dispatch(marks_send, marks_all, marks_a_send, marks_a_recv)

    cells = cells_ref[...]
    picks = []
    for b in range(2):
        here = jnp.where(
            lax.broadcasted_iota(jnp.int32, (samples, samples), 0) + b * samples == cells, 1.0, 0.0
        ).astype(jnp.bfloat16)
        pick = lax.dot_general(
            chosen, here, (((1,), (1,)), ((), ())), preferred_element_type=jnp.float32
        )
        picks.append(pick.astype(jnp.bfloat16))

    loads[3].wait()
    means = [0.0, 0.0, 0.0]
    for m0 in RANGE:
        q = [field[m0, :, m] for m in RANGE]
        a = [velocity[2, m0, :, m] for m in RANGE]
        means[2] = means[2] + jnp.sum(a[0] + a[1] + a[2] + a[3] + a[4], axis=0)
        q_left, a_left, q_right, a_right = (
            weighted(LEFT, q), weighted(LEFT, a), weighted(RIGHT, q), weighted(RIGHT, a)
        )
        left = upwind(shift(q_right, 1), shift(a_right, 1), q_left, a_left)
        right = upwind(q_right, a_right, shift(q_left, -1), shift(a_left, -1))
        f = [x * y for x, y in zip(q, a)]
        for k in RANGE:
            new_ref[m0, :, k] = q[k] - (
                weighted(INNER[k], f)
                + left * np.float32(EDGE_LEFT[k])
                + right * np.float32(EDGE_RIGHT[k])
            )
    for m0 in RANGE:
        a = [velocity[1, m0, m] for m in RANGE]
        means[1] = means[1] + jnp.sum(a[0] + a[1] + a[2] + a[3] + a[4], axis=0)
        f = [field[m0, m] * a[m] for m in RANGE]
        for k in RANGE:
            new_ref[m0, k] = new_ref[m0, k] - weighted(INNER[k], f)
    for j in RANGE:
        a = [velocity[0, m, j] for m in RANGE]
        means[0] = means[0] + jnp.sum(a[0] + a[1] + a[2] + a[3] + a[4], axis=0)
        f = [field[m, j] * a[m] for m in RANGE]
        for k in RANGE:
            new_ref[k, j] = new_ref[k, j] - weighted(INNER[k], f)
    points = P_SIZE**3
    for d in range(3):
        flat[2 * (points + d) : 2 * (points + d) + 2] = means[d] * np.float32(1.0 / points)

    arrive(marks_all, marks_a, marks_a_recv, marks_a_send)
    marks_b = gather(marks_all, marks_b_send, marks_b_recv)

    for copy, _, gets in halos[:2]:
        pl.when(gets)(copy.wait_recv)
    for j in RANGE:
        left = upwind(zero_before[0, j], zero_before[1, j], own_zero[0, j], own_zero[1, j])
        right = upwind(own_zero[2, j], own_zero[3, j], zero_after[0, j], zero_after[1, j])
        for k in RANGE:
            new_ref[k, j] = new_ref[k, j] - (
                left * np.float32(EDGE_LEFT[k]) + right * np.float32(EDGE_RIGHT[k])
            )
    for copy, _, gets in halos[2:]:
        pl.when(gets)(copy.wait_recv)
    second = lax.broadcasted_iota(jnp.int32, (P_SIZE, 2, field.shape[-1]), 1) == 1
    for m0 in RANGE:
        before = [swap(jnp.where(second, one_before[n, m0], own_one[2 + n, m0])) for n in range(2)]
        after = [swap(jnp.where(second, own_one[n, m0], one_after[n, m0])) for n in range(2)]
        left = upwind(before[0], before[1], own_one[0, m0], own_one[1, m0])
        right = upwind(own_one[2, m0], own_one[3, m0], after[0], after[1])
        for k in RANGE:
            value = new_ref[m0, k] - (
                left * np.float32(EDGE_LEFT[k]) + right * np.float32(EDGE_RIGHT[k])
            )
            new_ref[m0, k] = value
            for n in RANGE:
                point = (m0 * P_SIZE + k) * P_SIZE + n
                flat[2 * point : 2 * point + 2] = value[n]

    total = None
    for b in range(2):
        values = flat[pl.ds(b, points + 3, stride=2)].astype(jnp.bfloat16)
        part = lax.dot_general(
            picks[b], values, (((1,), (1,)), ((), ())), preferred_element_type=jnp.float32
        )
        total = part if total is None else total + part
    rows_send[...] = total.astype(jnp.bfloat16).reshape(rows_send.shape)
    rows_a = dispatch(rows_send, rows_all, rows_a_send, rows_a_recv)
    arrive(rows_all, rows_a, rows_a_recv, rows_a_send)
    rows_b = gather(rows_all, rows_b_send, rows_b_recv)
    for copy, sends, _ in halos:
        pl.when(sends)(copy.wait_send)
    for copy in marks_a + rows_a:
        copy.wait_send()
    gathered(marks_all, marks_b, marks_b_send, marks_b_recv)
    gathered(rows_all, rows_b, rows_b_send, rows_b_recv)


def train_kernel(
    per_chunk,
    new_ref, rows_all, marks_all, one, two, three, four, five,
    new_out, grad_one, grad_two, grad_three, grad_four, grad_five,
    copy_sem,
):
    copy = pltpu.make_async_copy(new_ref, new_out, copy_sem)
    copy.start()
    walls, spans = rows_all.shape[:2]
    weights = (one, two, three, four, five)
    grads = (grad_one, grad_two, grad_three, grad_four, grad_five)
    chunks = walls // per_chunk
    count = per_chunk * spans * CAP

    def chunk(number):
        picked = pl.ds(number * per_chunk, per_chunk)
        act = rows_all[picked].reshape(count, -1)
        wanted = marks_all[picked, :, 0:CAP].reshape(per_chunk, spans * CAP, -1).astype(jnp.float32)
        flags = marks_all[picked, :, CAP : 2 * CAP].reshape(per_chunk, spans * CAP, -1).astype(jnp.float32)
        scale = flags / jnp.maximum(jnp.sum(flags, axis=1, keepdims=True), 1.0)
        acts = [act]
        slopes = []
        for layer in weights[:-1]:
            pre = jnp.dot(act, layer[0], preferred_element_type=jnp.float32)
            sigma = 0.5 + 0.5 * jnp.tanh(0.5 * pre)
            hidden = pre * sigma
            slopes.append(sigma + hidden * (1.0 - sigma))
            act = hidden.astype(jnp.bfloat16)
            acts.append(act)
        output = jnp.dot(act, weights[-1][0], preferred_element_type=jnp.float32)
        error = scale * (output.reshape(wanted.shape) - wanted)
        error = error.reshape(count, -1).astype(jnp.bfloat16)
        for layer in range(4, -1, -1):
            grad = lax.dot_general(
                acts[layer], error, (((0,), (0,)), ((), ())), preferred_element_type=jnp.float32
            )
            if chunks == 1:
                grads[layer][0] = grad
            else:
                grads[layer][0] += grad
            if layer:
                back = lax.dot_general(
                    error, weights[layer][0], (((1,), (1,)), ((), ())), preferred_element_type=jnp.float32
                )
                error = (back * slopes[layer - 1]).astype(jnp.bfloat16)

    if chunks == 1:
        chunk(0)
    else:
        for grad in grads:
            grad[...] = jnp.zeros_like(grad)
        pl.loop(0, chunks)(chunk)
    copy.wait()


def local(spans, walls, field, velocity, cells, destination, targets, *weights):
    shape = field.shape
    samples = cells.shape[0]
    inside = (P_SIZE, P_SIZE, P_SIZE, shape[3] * shape[4], shape[5])
    faces = (P_SIZE, P_SIZE) + inside[3:]
    vmem = pl.BlockSpec(memory_space=pltpu.VMEM)
    anywhere = pl.BlockSpec(memory_space=pl.ANY)
    features = P_SIZE**3 + 3
    wide = targets.shape[1]
    dma = pltpu.SemaphoreType.DMA
    new_field, rows_all, marks_all = pl.pallas_call(
        functools.partial(section_kernel, spans, walls),
        out_shape=(
            jax.ShapeDtypeStruct(inside, jnp.float32),
            jax.ShapeDtypeStruct((walls, spans, CAP, features), jnp.bfloat16),
            jax.ShapeDtypeStruct((walls, spans, 2 * CAP, wide), jnp.bfloat16),
        ),
        in_specs=[anywhere, anywhere, vmem, vmem, vmem],
        out_specs=(vmem, vmem, vmem),
        scratch_shapes=[
            pltpu.VMEM(inside, jnp.float32),
            pltpu.VMEM((3,) + inside, jnp.float32),
            pltpu.VMEM((4,) + faces, jnp.float32),
            pltpu.VMEM((4,) + faces, jnp.float32),
            pltpu.VMEM((2,) + faces, jnp.float32),
            pltpu.VMEM((2,) + faces, jnp.float32),
            pltpu.VMEM((2,) + faces, jnp.float32),
            pltpu.VMEM((2,) + faces, jnp.float32),
            pltpu.VMEM((2 * features, shape[5]), jnp.float32),
            pltpu.VMEM((spans, CAP, features), jnp.bfloat16),
            pltpu.VMEM((spans, 2 * CAP, wide), jnp.bfloat16),
            dma((4,)), dma((4,)), dma((4,)),
            dma((spans,)), dma((spans,)), dma((walls,)), dma((walls,)),
            dma((spans,)), dma((spans,)), dma((walls,)), dma((walls,)),
        ],
        compiler_params=pltpu.CompilerParams(
            collective_id=0, has_side_effects=True, vmem_limit_bytes=48 * 1024 * 1024
        ),
        name="section",
    )(
        field.reshape(inside),
        velocity.reshape((3,) + inside),
        cells.reshape(1, samples),
        destination.reshape(1, samples),
        targets,
    )
    per_chunk = max(1, min(walls, 512 // (spans * CAP)))
    while walls % per_chunk:
        per_chunk -= 1
    outs = pl.pallas_call(
        functools.partial(train_kernel, per_chunk),
        out_shape=(jax.ShapeDtypeStruct(inside, jnp.float32),)
        + tuple(jax.ShapeDtypeStruct(x.shape, jnp.float32) for x in weights),
        in_specs=[anywhere] + [vmem] * 7,
        out_specs=(anywhere,) + (vmem,) * 5,
        scratch_shapes=[dma(())],
        compiler_params=pltpu.CompilerParams(vmem_limit_bytes=48 * 1024 * 1024),
        name="train",
    )(new_field, rows_all, marks_all, *weights)
    return (outs[0].reshape(shape),) + tuple(outs[1:])


def solution(mesh):
    in_specs = (
        P(None, None, None, "span", "wall", None),
        P(None, None, None, None, "span", "wall", None),
        P(("span", "wall")),
        P(("span", "wall"), None),
        P(("span", "wall"), None),
        P("span", None, None),
        P("span", None, None),
        P("span", None, None),
        P("span", None, None),
        P("span", None, None),
    )
    out_specs = (
        P(None, None, None, "span", "wall", None),
        P("span", None, None),
        P("span", None, None),
        P("span", None, None),
        P("span", None, None),
        P("span", None, None),
    )
    body = functools.partial(local, mesh.shape["span"], mesh.shape["wall"])
    return jax.shard_map(body, mesh=mesh, in_specs=in_specs, out_specs=out_specs, check_vma=False)
```

```python
import functools
import math

import jax
import jax.numpy as jnp
import numpy as np
from jax import lax
from jax.experimental import pallas as pl
from jax.experimental.pallas import tpu as pltpu
from jax.sharding import PartitionSpec as P

P_SIZE = 5
CAP = 16
MESH = pl.DeviceIdType.MESH


step_scale = 0.04


def legendre_pair(order, point):
    value_prev = 1.0
    value_now = point
    slope_prev = 0.0
    slope_now = 1.0
    for degree in range(1, order):
        value_next = ((2 * degree + 1) * point * value_now - degree * value_prev) / (degree + 1)
        slope_next = slope_prev + (2 * degree + 1) * value_now
        value_prev, value_now = (value_now, value_next)
        slope_prev, slope_now = (slope_now, slope_next)
    return (value_now, slope_now)


def gauss_nodes(count):
    found = []
    for index in range(count):
        guess = math.cos(math.pi * (index + 0.75) / (count + 0.5))
        for sweep in range(60):
            value, slope = legendre_pair(count, guess)
            guess = guess - value / slope
        found.append(guess)
    return sorted(found)


def fr_tables():
    nodes = gauss_nodes(P_SIZE)
    bary = []
    for j in range(P_SIZE):
        product = 1.0
        for m in range(P_SIZE):
            if m != j:
                product = product * (nodes[j] - nodes[m])
        bary.append(1.0 / product)
    deriv = [[0.0] * P_SIZE for row_index in range(P_SIZE)]
    for i in range(P_SIZE):
        for j in range(P_SIZE):
            if i != j:
                deriv[i][j] = bary[j] / bary[i] / (nodes[i] - nodes[j])
        deriv[i][i] = -sum((deriv[i][j] for j in range(P_SIZE) if j != i))

    def basis_at(point):
        values = []
        for j in range(P_SIZE):
            product = 1.0
            for m in range(P_SIZE):
                if m != j:
                    product = product * (point - nodes[m]) / (nodes[j] - nodes[m])
            values.append(product)
        return values

    left_value = basis_at(-1.0)
    right_value = basis_at(1.0)
    sign = (-1.0) ** P_SIZE
    slope_left = [
        0.5 * sign * (legendre_pair(P_SIZE, x)[1] - legendre_pair(P_SIZE - 1, x)[1]) for x in nodes
    ]
    slope_right = [-slope_left[P_SIZE - 1 - i] for i in range(P_SIZE)]
    inner = [
        [
            step_scale
            * (deriv[i][m] - slope_left[i] * left_value[m] - slope_right[i] * right_value[m])
            for m in range(P_SIZE)
        ]
        for i in range(P_SIZE)
    ]
    edge_left = [0.25 * step_scale * s for s in slope_left]
    edge_right = [0.25 * step_scale * s for s in slope_right]
    return inner, left_value, right_value, edge_left, edge_right


INNER, LEFT, RIGHT, EDGE_LEFT, EDGE_RIGHT = fr_tables()
RANGE = range(P_SIZE)


def weighted(table, parts):
    total = parts[0] * np.float32(table[0])
    for weight, part in zip(table[1:], parts[1:]):
        total = total + part * np.float32(weight)
    return total


def upwind(state_before, speed_before, state_after, speed_after):
    speed = speed_before + speed_after
    return speed * (state_before + state_after) - jnp.abs(speed) * (state_after - state_before)


def beside(x, y, row, other=None):
    other = row if other is None else other
    return jnp.concatenate([x[..., row : row + 1, :], y[..., other : other + 1, :]], axis=-2)


def shift(x, step):
    return jnp.concatenate([x[..., -step:], x[..., :-step]], axis=-1)


def section_kernel(
    spans, walls,
    field_hbm, velocity_hbm, cells_hbm, dest_hbm, targets_hbm,
    new_ref, rows_all, wanted_all, flags_all,
    field, velocity, cells_ref, dest_ref, targets_ref,
    own_zero, own_one, one_send, zero_before, zero_after, one_before, one_after,
    flat, rows_send, marks_send, marks_held,
    in_sems, halo_send, halo_recv,
    marks_a_send, marks_a_recv, wanted_b_send, wanted_b_recv, flags_b_send, flags_b_recv,
    rows_a_send, rows_a_recv, rows_b_send, rows_b_recv,
):
    i = lax.axis_index("span")
    w = lax.axis_index("wall")
    barrier = pltpu.get_barrier_semaphore()
    for d in range(1, spans):
        pl.semaphore_signal(barrier, inc=1, device_id={"span": lax.rem(i + d, spans)}, device_id_type=MESH)
    for d in range(1, walls):
        pl.semaphore_signal(barrier, inc=1, device_id={"wall": lax.rem(w + d, walls)}, device_id_type=MESH)

    loads = [pltpu.make_async_copy(field_hbm, field, in_sems.at[0])]
    for d in range(3):
        loads.append(pltpu.make_async_copy(velocity_hbm.at[d], velocity.at[d], in_sems.at[1 + d]))
    for number, (whole, ref) in enumerate(((dest_hbm, dest_ref), (targets_hbm, targets_ref), (cells_hbm, cells_ref))):
        loads.append(pltpu.make_async_copy(whole, ref, in_sems.at[4 + number]))
    for load in loads:
        load.start()

    for at_end, ref in ((i == 0, zero_before), (i == spans - 1, zero_after), (w == 0, one_before), (w == walls - 1, one_after)):
        @pl.when(at_end)
        def _(ref=ref):
            ref[...] = jnp.zeros_like(ref)

    loads[0].wait()
    loads[1].wait()
    for j in RANGE:
        q = [field[m, j] for m in RANGE]
        a = [velocity[0, m, j] for m in RANGE]
        own_zero[0, j] = weighted(LEFT, q)
        own_zero[1, j] = weighted(LEFT, a)
        own_zero[2, j] = weighted(RIGHT, q)
        own_zero[3, j] = weighted(RIGHT, a)
    loads[2].wait()
    for m0 in RANGE:
        q = [field[m0, m] for m in RANGE]
        a = [velocity[1, m0, m] for m in RANGE]
        own_one[0, m0] = weighted(LEFT, q)
        own_one[1, m0] = weighted(LEFT, a)
        own_one[2, m0] = weighted(RIGHT, q)
        own_one[3, m0] = weighted(RIGHT, a)
        one_send[0, m0] = beside(own_one[0, m0], own_one[1, m0], 0)
        one_send[1, m0] = beside(own_one[2, m0], own_one[3, m0], 1)

    pl.semaphore_wait(barrier, spans + walls - 2)

    def halo(number, axis, place, count, source, into, right):
        peer = jnp.minimum(place + 1, count - 1) if right else jnp.maximum(place - 1, 0)
        copy = pltpu.make_async_remote_copy(
            src_ref=source,
            dst_ref=into,
            send_sem=halo_send.at[number],
            recv_sem=halo_recv.at[number],
            device_id={axis: peer},
            device_id_type=MESH,
        )
        sends = place < count - 1 if right else place > 0
        gets = place > 0 if right else place < count - 1
        return copy, sends, gets

    halos = [
        halo(0, "span", i, spans, own_zero.at[2:4], zero_before, True),
        halo(1, "span", i, spans, own_zero.at[0:2], zero_after, False),
        halo(2, "wall", w, walls, one_send.at[1], one_before, True),
        halo(3, "wall", w, walls, one_send.at[0], one_after, False),
    ]
    for copy, sends, _ in halos:
        pl.when(sends)(copy.start)

    samples = dest_ref.shape[1]
    for load in loads[4:]:
        load.wait()
    dest = dest_ref[...]
    across = jnp.broadcast_to(dest, (samples, samples))
    down = jnp.transpose(across)
    earlier = lax.broadcasted_iota(jnp.int32, (samples, samples), 0) < lax.broadcasted_iota(jnp.int32, (samples, samples), 1)
    slot = jnp.sum(jnp.where(jnp.logical_and(across == down, earlier), 1.0, 0.0), axis=0, keepdims=True)
    position = dest * CAP + slot.astype(jnp.int32)
    places = spans * CAP
    chosen = jnp.where(
        lax.broadcasted_iota(jnp.int32, (places, samples), 0) == position, 1.0, 0.0
    ).astype(jnp.bfloat16)
    wanted = jnp.dot(chosen, targets_ref[...], preferred_element_type=jnp.float32)
    flags = jnp.dot(chosen, jnp.ones((samples, samples), jnp.bfloat16), preferred_element_type=jnp.float32)
    marks_send[:, 0:CAP] = wanted.astype(jnp.bfloat16).reshape(spans, CAP, -1)
    marks_send[:, CAP : 2 * CAP] = flags.astype(jnp.bfloat16).reshape(spans, CAP, -1)

    def dispatch(send, held, send_sems, recv_sems):
        copies = []
        for d in range(1, spans):
            peer = lax.rem(i + d, spans)
            copies.append(
                pltpu.make_async_remote_copy(
                    src_ref=send.at[peer],
                    dst_ref=held.at[i],
                    send_sem=send_sems.at[d],
                    recv_sem=recv_sems.at[d],
                    device_id={"span": peer},
                    device_id_type=MESH,
                )
            )
        for copy in copies:
            copy.start()
        held[i] = send[i]
        return copies

    def arrive(held, send_sems, recv_sems):
        for d in range(1, spans):
            source = lax.rem(i + spans - d, spans)
            pltpu.make_async_remote_copy(
                src_ref=held.at[source],
                dst_ref=held.at[source],
                send_sem=send_sems.at[d],
                recv_sem=recv_sems.at[d],
                device_id={"span": source},
                device_id_type=MESH,
            ).wait_recv()

    def gather(held, send_sems, recv_sems):
        copies = []
        for d in range(1, walls):
            copies.append(
                pltpu.make_async_remote_copy(
                    src_ref=held.at[w],
                    dst_ref=held.at[w],
                    send_sem=send_sems.at[d],
                    recv_sem=recv_sems.at[d],
                    device_id={"wall": lax.rem(w + d, walls)},
                    device_id_type=MESH,
                )
            )
        for copy in copies:
            copy.start()
        return copies

    def gathered(held, copies, send_sems, recv_sems):
        for d in range(1, walls):
            source = lax.rem(w + walls - d, walls)
            pltpu.make_async_remote_copy(
                src_ref=held.at[source],
                dst_ref=held.at[source],
                send_sem=send_sems.at[d],
                recv_sem=recv_sems.at[d],
                device_id={"wall": source},
                device_id_type=MESH,
            ).wait_recv()
        for copy in copies:
            copy.wait_send()

    marks_a = dispatch(marks_send, marks_held, marks_a_send, marks_a_recv)

    cells = cells_ref[...]
    picks = []
    for b in range(2):
        here = jnp.where(
            lax.broadcasted_iota(jnp.int32, (samples, samples), 0) + b * samples == cells, 1.0, 0.0
        ).astype(jnp.bfloat16)
        pick = lax.dot_general(
            chosen, here, (((1,), (1,)), ((), ())), preferred_element_type=jnp.float32
        )
        picks.append(pick.astype(jnp.bfloat16))

    loads[3].wait()
    means = [0.0, 0.0, 0.0]
    for m0 in RANGE:
        q = [field[m0, :, m] for m in RANGE]
        a = [velocity[2, m0, :, m] for m in RANGE]
        means[2] = means[2] + jnp.sum(a[0] + a[1] + a[2] + a[3] + a[4], axis=0)
        q_left, a_left, q_right, a_right = (
            weighted(LEFT, q), weighted(LEFT, a), weighted(RIGHT, q), weighted(RIGHT, a)
        )
        left = upwind(shift(q_right, 1), shift(a_right, 1), q_left, a_left)
        right = upwind(q_right, a_right, shift(q_left, -1), shift(a_left, -1))
        f = [x * y for x, y in zip(q, a)]
        for k in RANGE:
            new_ref[m0, :, k] = q[k] - (
                weighted(INNER[k], f)
                + left * np.float32(EDGE_LEFT[k])
                + right * np.float32(EDGE_RIGHT[k])
            )
    for m0 in RANGE:
        a = [velocity[1, m0, m] for m in RANGE]
        means[1] = means[1] + jnp.sum(a[0] + a[1] + a[2] + a[3] + a[4], axis=0)
        f = [field[m0, m] * a[m] for m in RANGE]
        for k in RANGE:
            new_ref[m0, k] = new_ref[m0, k] - weighted(INNER[k], f)
    for j in RANGE:
        a = [velocity[0, m, j] for m in RANGE]
        means[0] = means[0] + jnp.sum(a[0] + a[1] + a[2] + a[3] + a[4], axis=0)
        f = [field[m, j] * a[m] for m in RANGE]
        for k in RANGE:
            new_ref[k, j] = new_ref[k, j] - weighted(INNER[k], f)
    points = P_SIZE**3
    for d in range(3):
        flat[2 * (points + d) : 2 * (points + d) + 2] = means[d] * np.float32(1.0 / points)

    arrive(marks_held, marks_a_send, marks_a_recv)
    wanted_all[w] = marks_held[:, 0:CAP].reshape(places, -1)
    flags_here = marks_held[:, CAP : 2 * CAP].reshape(places, -1).astype(jnp.float32)
    flags_all[w] = jnp.transpose(flags_here)[0:CAP].astype(jnp.bfloat16)
    wanted_b = gather(wanted_all, wanted_b_send, wanted_b_recv)
    flags_b = gather(flags_all, flags_b_send, flags_b_recv)

    for copy, _, gets in halos[:2]:
        pl.when(gets)(copy.wait_recv)
    for j in RANGE:
        left = upwind(zero_before[0, j], zero_before[1, j], own_zero[0, j], own_zero[1, j])
        right = upwind(own_zero[2, j], own_zero[3, j], zero_after[0, j], zero_after[1, j])
        for k in RANGE:
            new_ref[k, j] = new_ref[k, j] - (
                left * np.float32(EDGE_LEFT[k]) + right * np.float32(EDGE_RIGHT[k])
            )
    for copy, _, gets in halos[2:]:
        pl.when(gets)(copy.wait_recv)
    for m0 in RANGE:
        before = [beside(one_before[m0], own_one[2 + n, m0], n, 0) for n in range(2)]
        after = [beside(own_one[n, m0], one_after[m0], 1, n) for n in range(2)]
        left = upwind(before[0], before[1], own_one[0, m0], own_one[1, m0])
        right = upwind(own_one[2, m0], own_one[3, m0], after[0], after[1])
        for k in RANGE:
            value = new_ref[m0, k] - (
                left * np.float32(EDGE_LEFT[k]) + right * np.float32(EDGE_RIGHT[k])
            )
            new_ref[m0, k] = value
            for n in RANGE:
                point = (m0 * P_SIZE + k) * P_SIZE + n
                flat[2 * point : 2 * point + 2] = value[n]

    total = None
    for b in range(2):
        values = flat[pl.ds(b, points + 3, stride=2)].astype(jnp.bfloat16)
        part = lax.dot_general(
            picks[b], values, (((1,), (1,)), ((), ())), preferred_element_type=jnp.float32
        )
        total = part if total is None else total + part
    rows_send[...] = total.astype(jnp.bfloat16).reshape(rows_send.shape)
    rows_a = dispatch(rows_send, rows_all.at[w], rows_a_send, rows_a_recv)
    arrive(rows_all.at[w], rows_a_send, rows_a_recv)
    rows_b = gather(rows_all, rows_b_send, rows_b_recv)
    for copy, sends, _ in halos:
        pl.when(sends)(copy.wait_send)
    for copy in marks_a + rows_a:
        copy.wait_send()
    gathered(wanted_all, wanted_b, wanted_b_send, wanted_b_recv)
    gathered(flags_all, flags_b, flags_b_send, flags_b_recv)
    gathered(rows_all, rows_b, rows_b_send, rows_b_recv)


def train_kernel(
    per_chunk,
    new_ref, rows_all, wanted_all, flags_all, one, two, three, four, five,
    new_out, out_one, out_two, out_three, out_four, out_five,
    grad_one, grad_two, grad_three, grad_four, grad_five, sems,
):
    copies = [pltpu.make_async_copy(new_ref, new_out, sems.at[5])]
    copies[0].start()
    walls, spans = rows_all.shape[:2]
    weights = (one, two, three, four, five)
    grads = (grad_one, grad_two, grad_three, grad_four, grad_five)
    outs = (out_one, out_two, out_three, out_four, out_five)
    chunks = walls // per_chunk
    places = spans * CAP
    count = per_chunk * places

    def leave(layer):
        copy = pltpu.make_async_copy(grads[layer], outs[layer], sems.at[layer])
        copy.start()
        copies.append(copy)

    def chunk(number):
        first = number * per_chunk
        act = rows_all[pl.ds(first, per_chunk)].reshape(count, -1)
        wanted = wanted_all[pl.ds(first, per_chunk)].reshape(count, -1).astype(jnp.float32)
        wide = wanted.shape[1]
        scales = []
        for n in range(per_chunk):
            flags = flags_all[first + n].astype(jnp.float32)[0:1]
            scale = flags / jnp.maximum(jnp.sum(flags, axis=1, keepdims=True), 1.0)
            scales.append(jnp.transpose(jnp.broadcast_to(scale, (wide, places))))
        scale = scales[0] if per_chunk == 1 else jnp.concatenate(scales, axis=0)
        acts = [act]
        slopes = []
        for layer in weights[:-1]:
            pre = jnp.dot(act, layer[0], preferred_element_type=jnp.float32)
            sigma = 0.5 + 0.5 * jnp.tanh(0.5 * pre)
            hidden = pre * sigma
            slopes.append(sigma + hidden * (1.0 - sigma))
            act = hidden.astype(jnp.bfloat16)
            acts.append(act)
        output = jnp.dot(act, weights[-1][0], preferred_element_type=jnp.float32)
        error = (scale * (output - wanted)).astype(jnp.bfloat16)
        for layer in range(4, -1, -1):
            grad = lax.dot_general(
                acts[layer], error, (((0,), (0,)), ((), ())), preferred_element_type=jnp.float32
            )
            if chunks == 1:
                grads[layer][0] = grad
                leave(layer)
            else:
                grads[layer][0] += grad
            if layer:
                back = lax.dot_general(
                    error, weights[layer][0], (((1,), (1,)), ((), ())), preferred_element_type=jnp.float32
                )
                error = (back * slopes[layer - 1]).astype(jnp.bfloat16)

    if chunks == 1:
        chunk(0)
    else:
        for grad in grads:
            grad[...] = jnp.zeros_like(grad)
        pl.loop(0, chunks)(chunk)
        for layer in range(5):
            leave(layer)
    for copy in copies:
        copy.wait()


def local(spans, walls, field, velocity, cells, destination, targets, *weights):
    shape = field.shape
    samples = cells.shape[0]
    inside = (P_SIZE, P_SIZE, P_SIZE, shape[3] * shape[4], shape[5])
    faces = (P_SIZE, P_SIZE) + inside[3:]
    vmem = pl.BlockSpec(memory_space=pltpu.VMEM)
    anywhere = pl.BlockSpec(memory_space=pl.ANY)
    hbm = pl.BlockSpec(memory_space=pltpu.HBM)
    features = P_SIZE**3 + 3
    wide = targets.shape[1]
    dma = pltpu.SemaphoreType.DMA
    new_field, *received = pl.pallas_call(
        functools.partial(section_kernel, spans, walls),
        out_shape=(
            jax.ShapeDtypeStruct(inside, jnp.float32),
            jax.ShapeDtypeStruct((walls, spans, CAP, features), jnp.bfloat16),
            jax.ShapeDtypeStruct((walls, spans * CAP, wide), jnp.bfloat16),
            jax.ShapeDtypeStruct((walls, CAP, spans * CAP), jnp.bfloat16),
        ),
        in_specs=[hbm] * 5,
        out_specs=(vmem,) * 4,
        scratch_shapes=[
            pltpu.VMEM(inside, jnp.float32),
            pltpu.VMEM((3,) + inside, jnp.float32),
            pltpu.VMEM((1, samples), jnp.int32),
            pltpu.VMEM((1, samples), jnp.int32),
            pltpu.VMEM(targets.shape, jnp.bfloat16),
            pltpu.VMEM((4,) + faces, jnp.float32),
            pltpu.VMEM((4,) + faces, jnp.float32),
            pltpu.VMEM((2,) + faces, jnp.float32),
            pltpu.VMEM((2,) + faces, jnp.float32),
            pltpu.VMEM((2,) + faces, jnp.float32),
            pltpu.VMEM(faces, jnp.float32),
            pltpu.VMEM(faces, jnp.float32),
            pltpu.VMEM((2 * features, shape[5]), jnp.float32),
            pltpu.VMEM((spans, CAP, features), jnp.bfloat16),
            pltpu.VMEM((spans, 2 * CAP, wide), jnp.bfloat16),
            pltpu.VMEM((spans, 2 * CAP, wide), jnp.bfloat16),
            dma((7,)), dma((4,)), dma((4,)),
            dma((spans,)), dma((spans,)), dma((walls,)), dma((walls,)), dma((walls,)), dma((walls,)),
            dma((spans,)), dma((spans,)), dma((walls,)), dma((walls,)),
        ],
        compiler_params=pltpu.CompilerParams(
            collective_id=0, has_side_effects=True, vmem_limit_bytes=48 * 1024 * 1024
        ),
        name="section",
    )(
        *(
            pltpu.with_memory_space_constraint(x, pltpu.HBM)
            for x in (
                field.reshape(inside),
                velocity.reshape((3,) + inside),
                cells.reshape(1, samples),
                destination.reshape(1, samples),
                targets,
            )
        )
    )
    per_chunk = max(1, min(walls, 512 // (spans * CAP)))
    while walls % per_chunk:
        per_chunk -= 1
    outs = pl.pallas_call(
        functools.partial(train_kernel, per_chunk),
        out_shape=(jax.ShapeDtypeStruct(inside, jnp.float32),)
        + tuple(jax.ShapeDtypeStruct(x.shape, jnp.float32) for x in weights),
        in_specs=[anywhere] + [vmem] * 8,
        out_specs=(anywhere,) * 6,
        scratch_shapes=[pltpu.VMEM(x.shape, jnp.float32) for x in weights] + [dma((6,))],
        compiler_params=pltpu.CompilerParams(vmem_limit_bytes=48 * 1024 * 1024),
        name="train",
    )(new_field, *received, *weights)
    return (outs[0].reshape(shape),) + tuple(outs[1:])


def solution(mesh):
    in_specs = (
        P(None, None, None, "span", "wall", None),
        P(None, None, None, None, "span", "wall", None),
        P(("span", "wall")),
        P(("span", "wall"), None),
        P(("span", "wall"), None),
        P("span", None, None),
        P("span", None, None),
        P("span", None, None),
        P("span", None, None),
        P("span", None, None),
    )
    out_specs = (
        P(None, None, None, "span", "wall", None),
        P("span", None, None),
        P("span", None, None),
        P("span", None, None),
        P("span", None, None),
        P("span", None, None),
    )
    body = functools.partial(local, mesh.shape["span"], mesh.shape["wall"])
    return jax.shard_map(body, mesh=mesh, in_specs=in_specs, out_specs=out_specs, check_vma=False)
```

```python
import functools
import math

import jax
import jax.numpy as jnp
import numpy as np
from jax import lax
from jax.experimental import pallas as pl
from jax.experimental.pallas import tpu as pltpu
from jax.sharding import PartitionSpec as P

P_SIZE = 5
CAP = 16
MESH = pl.DeviceIdType.MESH


step_scale = 0.04


def legendre_pair(order, point):
    value_prev = 1.0
    value_now = point
    slope_prev = 0.0
    slope_now = 1.0
    for degree in range(1, order):
        value_next = ((2 * degree + 1) * point * value_now - degree * value_prev) / (degree + 1)
        slope_next = slope_prev + (2 * degree + 1) * value_now
        value_prev, value_now = (value_now, value_next)
        slope_prev, slope_now = (slope_now, slope_next)
    return (value_now, slope_now)


def gauss_nodes(count):
    found = []
    for index in range(count):
        guess = math.cos(math.pi * (index + 0.75) / (count + 0.5))
        for sweep in range(60):
            value, slope = legendre_pair(count, guess)
            guess = guess - value / slope
        found.append(guess)
    return sorted(found)


def fr_tables():
    nodes = gauss_nodes(P_SIZE)
    bary = []
    for j in range(P_SIZE):
        product = 1.0
        for m in range(P_SIZE):
            if m != j:
                product = product * (nodes[j] - nodes[m])
        bary.append(1.0 / product)
    deriv = [[0.0] * P_SIZE for row_index in range(P_SIZE)]
    for i in range(P_SIZE):
        for j in range(P_SIZE):
            if i != j:
                deriv[i][j] = bary[j] / bary[i] / (nodes[i] - nodes[j])
        deriv[i][i] = -sum((deriv[i][j] for j in range(P_SIZE) if j != i))

    def basis_at(point):
        values = []
        for j in range(P_SIZE):
            product = 1.0
            for m in range(P_SIZE):
                if m != j:
                    product = product * (point - nodes[m]) / (nodes[j] - nodes[m])
            values.append(product)
        return values

    left_value = basis_at(-1.0)
    right_value = basis_at(1.0)
    sign = (-1.0) ** P_SIZE
    slope_left = [
        0.5 * sign * (legendre_pair(P_SIZE, x)[1] - legendre_pair(P_SIZE - 1, x)[1]) for x in nodes
    ]
    slope_right = [-slope_left[P_SIZE - 1 - i] for i in range(P_SIZE)]
    inner = [
        [
            step_scale
            * (deriv[i][m] - slope_left[i] * left_value[m] - slope_right[i] * right_value[m])
            for m in range(P_SIZE)
        ]
        for i in range(P_SIZE)
    ]
    edge_left = [0.25 * step_scale * s for s in slope_left]
    edge_right = [0.25 * step_scale * s for s in slope_right]
    return inner, left_value, right_value, edge_left, edge_right


INNER, LEFT, RIGHT, EDGE_LEFT, EDGE_RIGHT = fr_tables()
RANGE = range(P_SIZE)


def weighted(table, parts):
    total = parts[0] * np.float32(table[0])
    for weight, part in zip(table[1:], parts[1:]):
        total = total + part * np.float32(weight)
    return total


def upwind(state_before, speed_before, state_after, speed_after):
    speed = speed_before + speed_after
    return speed * (state_before + state_after) - jnp.abs(speed) * (state_after - state_before)


def beside(x, y, row, other=None):
    other = row if other is None else other
    return jnp.concatenate([x[..., row : row + 1, :], y[..., other : other + 1, :]], axis=-2)


def paired(place, d):
    bit = 1
    while bit <= d:
        if d & bit:
            place = place + bit * (1 - 2 * lax.rem(lax.div(place, bit), 2))
        bit *= 2
    return place


def is_full(spans, samples):
    return spans * CAP == samples


def shift(x, step):
    return jnp.concatenate([x[..., -step:], x[..., :-step]], axis=-1)


def section_kernel(
    spans, walls,
    field_hbm, velocity_hbm, cells_hbm, dest_hbm, targets_hbm,
    new_ref, rows_all, marks_all,
    field, velocity, cells_ref, dest_ref, targets_ref,
    own_zero, own_one, one_send, zero_before, zero_after, one_before, one_after,
    flat, rows_send, marks_send,
    in_sems, halo_send, halo_recv,
    marks_sems, marks_wall_sems, rows_sems, rows_wall_sems,
):
    i = lax.axis_index("span")
    w = lax.axis_index("wall")
    barrier = pltpu.get_barrier_semaphore()
    for d in range(1, spans):
        pl.semaphore_signal(barrier, inc=1, device_id={"span": lax.rem(i + d, spans)}, device_id_type=MESH)
    for d in range(1, walls):
        pl.semaphore_signal(barrier, inc=1, device_id={"wall": lax.rem(w + d, walls)}, device_id_type=MESH)

    loads = [pltpu.make_async_copy(field_hbm, field, in_sems.at[0])]
    for d in range(3):
        loads.append(pltpu.make_async_copy(velocity_hbm.at[d], velocity.at[d], in_sems.at[1 + d]))
    for number, (whole, ref) in enumerate(((dest_hbm, dest_ref), (targets_hbm, targets_ref), (cells_hbm, cells_ref))):
        loads.append(pltpu.make_async_copy(whole, ref, in_sems.at[4 + number]))
    for load in loads:
        load.start()

    for at_end, ref in ((i == 0, zero_before), (i == spans - 1, zero_after), (w == 0, one_before), (w == walls - 1, one_after)):
        @pl.when(at_end)
        def _(ref=ref):
            ref[...] = jnp.zeros_like(ref)

    loads[0].wait()
    loads[1].wait()
    for j in RANGE:
        q = [field[m, j] for m in RANGE]
        a = [velocity[0, m, j] for m in RANGE]
        own_zero[0, j] = weighted(LEFT, q)
        own_zero[1, j] = weighted(LEFT, a)
        own_zero[2, j] = weighted(RIGHT, q)
        own_zero[3, j] = weighted(RIGHT, a)
    loads[2].wait()
    for m0 in RANGE:
        q = [field[m0, m] for m in RANGE]
        a = [velocity[1, m0, m] for m in RANGE]
        own_one[0, m0] = weighted(LEFT, q)
        own_one[1, m0] = weighted(LEFT, a)
        own_one[2, m0] = weighted(RIGHT, q)
        own_one[3, m0] = weighted(RIGHT, a)
        one_send[0, m0] = beside(own_one[0, m0], own_one[1, m0], 0)
        one_send[1, m0] = beside(own_one[2, m0], own_one[3, m0], 1)

    pl.semaphore_wait(barrier, spans + walls - 2)

    def halo(number, axis, place, count, source, into, right):
        peer = jnp.minimum(place + 1, count - 1) if right else jnp.maximum(place - 1, 0)
        copy = pltpu.make_async_remote_copy(
            src_ref=source,
            dst_ref=into,
            send_sem=halo_send.at[number],
            recv_sem=halo_recv.at[number],
            device_id={axis: peer},
            device_id_type=MESH,
        )
        sends = place < count - 1 if right else place > 0
        gets = place > 0 if right else place < count - 1
        return copy, sends, gets

    halos = [
        halo(0, "span", i, spans, own_zero.at[2:4], zero_before, True),
        halo(1, "span", i, spans, own_zero.at[0:2], zero_after, False),
        halo(2, "wall", w, walls, one_send.at[1], one_before, True),
        halo(3, "wall", w, walls, one_send.at[0], one_after, False),
    ]
    for copy, sends, _ in halos:
        pl.when(sends)(copy.start)

    samples = dest_ref.shape[1]
    for load in loads[4:]:
        load.wait()
    dest = dest_ref[...]
    across = jnp.broadcast_to(dest, (samples, samples))
    down = jnp.transpose(across)
    earlier = lax.broadcasted_iota(jnp.int32, (samples, samples), 0) < lax.broadcasted_iota(jnp.int32, (samples, samples), 1)
    slot = jnp.sum(jnp.where(jnp.logical_and(across == down, earlier), 1.0, 0.0), axis=0, keepdims=True)
    position = dest * CAP + slot.astype(jnp.int32)
    places = spans * CAP
    chosen = jnp.where(
        lax.broadcasted_iota(jnp.int32, (places, samples), 0) == position, 1.0, 0.0
    ).astype(jnp.bfloat16)
    wanted = jnp.dot(chosen, targets_ref[...], preferred_element_type=jnp.float32)
    marks_send[:, 0:CAP] = wanted.astype(jnp.bfloat16).reshape(spans, CAP, -1)
    if not is_full(spans, samples):
        flags = jnp.dot(chosen, jnp.ones((samples, samples), jnp.bfloat16), preferred_element_type=jnp.float32)
        marks_send[:, CAP : 2 * CAP] = flags.astype(jnp.bfloat16).reshape(spans, CAP, -1)

    groups = min(spans, 8)
    size = spans // groups

    def group_of(held, wall, g):
        return held.at[wall, pl.ds(paired(lax.div(i, size), g) * size, size)]

    def dispatch(send, held, sems, wall_sems):
        copies = [
            pltpu.make_async_remote_copy(
                src_ref=send.at[paired(i, d)],
                dst_ref=held.at[w, i],
                send_sem=sems.at[0, d],
                recv_sem=sems.at[1, d],
                device_id={"span": paired(i, d)},
                device_id_type=MESH,
            )
            for d in range(1, spans)
        ]
        for copy in copies:
            copy.start()
        held[w, i] = send[i]
        if size == 1:
            copies = copies + forward(held, wall_sems, 0)
        return copies

    def forward(held, sems, g):
        place = group_of(held, w, g)
        copies = [
            pltpu.make_async_remote_copy(
                src_ref=place,
                dst_ref=place,
                send_sem=sems.at[0, n, g],
                recv_sem=sems.at[1, n, g],
                device_id={"wall": paired(w, n)},
                device_id_type=MESH,
            )
            for n in range(1, walls)
        ]
        for copy in copies:
            copy.start()
        return copies

    def pass_on(held, sems, wall_sems):
        copies = []
        for d in range(1, spans):
            source = paired(i, d)
            pltpu.make_async_remote_copy(
                src_ref=held.at[w, source],
                dst_ref=held.at[w, source],
                send_sem=sems.at[0, d],
                recv_sem=sems.at[1, d],
                device_id={"span": source},
                device_id_type=MESH,
            ).wait_recv()
            if (d + 1) % size == 0:
                copies += forward(held, wall_sems, d // size)
        return copies

    def finish(held, sems):
        for g in range(groups):
            for n in range(1, walls):
                place = group_of(held, paired(w, n), g)
                pltpu.make_async_remote_copy(
                    src_ref=place,
                    dst_ref=place,
                    send_sem=sems.at[0, n, g],
                    recv_sem=sems.at[1, n, g],
                    device_id={"wall": paired(w, n)},
                    device_id_type=MESH,
                ).wait_recv()

    sent = dispatch(marks_send, marks_all, marks_sems, marks_wall_sems)

    cells = cells_ref[...]
    picks = []
    for b in range(2):
        here = jnp.where(
            lax.broadcasted_iota(jnp.int32, (samples, samples), 0) + b * samples == cells, 1.0, 0.0
        ).astype(jnp.bfloat16)
        pick = lax.dot_general(
            chosen, here, (((1,), (1,)), ((), ())), preferred_element_type=jnp.float32
        )
        picks.append(pick.astype(jnp.bfloat16))

    loads[3].wait()
    means = [0.0, 0.0, 0.0]
    for m0 in RANGE:
        q = [field[m0, :, m] for m in RANGE]
        a = [velocity[2, m0, :, m] for m in RANGE]
        means[2] = means[2] + jnp.sum(a[0] + a[1] + a[2] + a[3] + a[4], axis=0)
        q_left, a_left, q_right, a_right = (
            weighted(LEFT, q), weighted(LEFT, a), weighted(RIGHT, q), weighted(RIGHT, a)
        )
        left = upwind(shift(q_right, 1), shift(a_right, 1), q_left, a_left)
        right = upwind(q_right, a_right, shift(q_left, -1), shift(a_left, -1))
        f = [x * y for x, y in zip(q, a)]
        for k in RANGE:
            new_ref[m0, :, k] = q[k] - (
                weighted(INNER[k], f)
                + left * np.float32(EDGE_LEFT[k])
                + right * np.float32(EDGE_RIGHT[k])
            )
    for m0 in RANGE:
        a = [velocity[1, m0, m] for m in RANGE]
        means[1] = means[1] + jnp.sum(a[0] + a[1] + a[2] + a[3] + a[4], axis=0)
        f = [field[m0, m] * a[m] for m in RANGE]
        for k in RANGE:
            new_ref[m0, k] = new_ref[m0, k] - weighted(INNER[k], f)
    for j in RANGE:
        a = [velocity[0, m, j] for m in RANGE]
        means[0] = means[0] + jnp.sum(a[0] + a[1] + a[2] + a[3] + a[4], axis=0)
        f = [field[m, j] * a[m] for m in RANGE]
        for k in RANGE:
            new_ref[k, j] = new_ref[k, j] - weighted(INNER[k], f)
    points = P_SIZE**3
    for d in range(3):
        flat[2 * (points + d) : 2 * (points + d) + 2] = means[d] * np.float32(1.0 / points)

    sent += pass_on(marks_all, marks_sems, marks_wall_sems)

    for copy, _, gets in halos[:2]:
        pl.when(gets)(copy.wait_recv)
    for j in RANGE:
        left = upwind(zero_before[0, j], zero_before[1, j], own_zero[0, j], own_zero[1, j])
        right = upwind(own_zero[2, j], own_zero[3, j], zero_after[0, j], zero_after[1, j])
        for k in RANGE:
            new_ref[k, j] = new_ref[k, j] - (
                left * np.float32(EDGE_LEFT[k]) + right * np.float32(EDGE_RIGHT[k])
            )
    for copy, _, gets in halos[2:]:
        pl.when(gets)(copy.wait_recv)
    for m0 in RANGE:
        before = [beside(one_before[m0], own_one[2 + n, m0], n, 0) for n in range(2)]
        after = [beside(own_one[n, m0], one_after[m0], 1, n) for n in range(2)]
        left = upwind(before[0], before[1], own_one[0, m0], own_one[1, m0])
        right = upwind(own_one[2, m0], own_one[3, m0], after[0], after[1])
        for k in RANGE:
            value = new_ref[m0, k] - (
                left * np.float32(EDGE_LEFT[k]) + right * np.float32(EDGE_RIGHT[k])
            )
            new_ref[m0, k] = value
            for n in RANGE:
                point = (m0 * P_SIZE + k) * P_SIZE + n
                flat[2 * point : 2 * point + 2] = value[n]

    total = None
    for b in range(2):
        values = flat[pl.ds(b, points + 3, stride=2)].astype(jnp.bfloat16)
        part = lax.dot_general(
            picks[b], values, (((1,), (1,)), ((), ())), preferred_element_type=jnp.float32
        )
        total = part if total is None else total + part
    rows_send[...] = total.astype(jnp.bfloat16).reshape(rows_send.shape)
    sent += dispatch(rows_send, rows_all, rows_sems, rows_wall_sems)
    sent += pass_on(rows_all, rows_sems, rows_wall_sems)
    for copy, sends, _ in halos:
        pl.when(sends)(copy.wait_send)
    for copy in sent:
        copy.wait_send()
    finish(marks_all, marks_wall_sems)
    finish(rows_all, rows_wall_sems)


def train_kernel(
    per_chunk, full,
    new_ref, rows_all, marks_all, one, two, three, four, five,
    new_out, out_one, out_two, out_three, out_four, out_five,
    grad_one, grad_two, grad_three, grad_four, grad_five, sems,
):
    copies = [pltpu.make_async_copy(new_ref, new_out, sems.at[5])]
    copies[0].start()
    walls, spans = rows_all.shape[:2]
    weights = (one, two, three, four, five)
    grads = (grad_one, grad_two, grad_three, grad_four, grad_five)
    outs = (out_one, out_two, out_three, out_four, out_five)
    chunks = walls // per_chunk
    places = spans * CAP
    count = per_chunk * places

    def leave(layer):
        copy = pltpu.make_async_copy(grads[layer], outs[layer], sems.at[layer])
        copy.start()
        copies.append(copy)

    def chunk(number):
        first = number * per_chunk
        act = rows_all[pl.ds(first, per_chunk)].reshape(count, -1)
        picked = marks_all.at[pl.ds(first, per_chunk)]
        wanted = picked[:, :, 0:CAP].reshape(count, -1).astype(jnp.float32)
        if full:
            scale = np.float32(1.0 / places)
        else:
            flags = picked[:, :, CAP : 2 * CAP].reshape(per_chunk, places, -1).astype(jnp.float32)
            scale = flags / jnp.maximum(jnp.sum(flags, axis=1, keepdims=True), 1.0)
            scale = scale.reshape(count, -1)
        acts = [act]
        slopes = []
        for layer in weights[:-1]:
            pre = jnp.dot(act, layer[0], preferred_element_type=jnp.float32)
            sigma = 0.5 + 0.5 * jnp.tanh(0.5 * pre)
            hidden = pre * sigma
            slopes.append(sigma + hidden * (1.0 - sigma))
            act = hidden.astype(jnp.bfloat16)
            acts.append(act)
        output = jnp.dot(act, weights[-1][0], preferred_element_type=jnp.float32)
        error = (scale * (output - wanted)).astype(jnp.bfloat16)
        for layer in range(4, -1, -1):
            grad = lax.dot_general(
                acts[layer], error, (((0,), (0,)), ((), ())), preferred_element_type=jnp.float32
            )
            if chunks == 1:
                grads[layer][0] = grad
                leave(layer)
            else:
                grads[layer][0] += grad
            if layer:
                back = lax.dot_general(
                    error, weights[layer][0], (((1,), (1,)), ((), ())), preferred_element_type=jnp.float32
                )
                error = (back * slopes[layer - 1]).astype(jnp.bfloat16)

    if chunks == 1:
        chunk(0)
    else:
        for grad in grads:
            grad[...] = jnp.zeros_like(grad)
        pl.loop(0, chunks)(chunk)
        for layer in range(5):
            leave(layer)
    for copy in copies:
        copy.wait()


def local(spans, walls, field, velocity, cells, destination, targets, *weights):
    shape = field.shape
    samples = cells.shape[0]
    inside = (P_SIZE, P_SIZE, P_SIZE, shape[3] * shape[4], shape[5])
    faces = (P_SIZE, P_SIZE) + inside[3:]
    vmem = pl.BlockSpec(memory_space=pltpu.VMEM)
    anywhere = pl.BlockSpec(memory_space=pl.ANY)
    hbm = pl.BlockSpec(memory_space=pltpu.HBM)
    features = P_SIZE**3 + 3
    wide = targets.shape[1]
    full = is_full(spans, samples)
    marks = CAP if full else 2 * CAP
    dma = pltpu.SemaphoreType.DMA
    new_field, *received = pl.pallas_call(
        functools.partial(section_kernel, spans, walls),
        out_shape=(
            jax.ShapeDtypeStruct(inside, jnp.float32),
            jax.ShapeDtypeStruct((walls, spans, CAP, features), jnp.bfloat16),
            jax.ShapeDtypeStruct((walls, spans, marks, wide), jnp.bfloat16),
        ),
        in_specs=[hbm] * 5,
        out_specs=(vmem,) * 3,
        scratch_shapes=[
            pltpu.VMEM(inside, jnp.float32),
            pltpu.VMEM((3,) + inside, jnp.float32),
            pltpu.VMEM((1, samples), jnp.int32),
            pltpu.VMEM((1, samples), jnp.int32),
            pltpu.VMEM(targets.shape, jnp.bfloat16),
            pltpu.VMEM((4,) + faces, jnp.float32),
            pltpu.VMEM((4,) + faces, jnp.float32),
            pltpu.VMEM((2,) + faces, jnp.float32),
            pltpu.VMEM((2,) + faces, jnp.float32),
            pltpu.VMEM((2,) + faces, jnp.float32),
            pltpu.VMEM(faces, jnp.float32),
            pltpu.VMEM(faces, jnp.float32),
            pltpu.VMEM((2 * features, shape[5]), jnp.float32),
            pltpu.VMEM((spans, CAP, features), jnp.bfloat16),
            pltpu.VMEM((spans, marks, wide), jnp.bfloat16),
            dma((7,)), dma((4,)), dma((4,)),
            dma((2, spans)), dma((2, walls, min(spans, 8))), dma((2, spans)), dma((2, walls, min(spans, 8))),
        ],
        compiler_params=pltpu.CompilerParams(
            collective_id=0, has_side_effects=True, vmem_limit_bytes=48 * 1024 * 1024
        ),
        name="section",
    )(
        *(
            pltpu.with_memory_space_constraint(x, pltpu.HBM)
            for x in (
                field.reshape(inside),
                velocity.reshape((3,) + inside),
                cells.reshape(1, samples),
                destination.reshape(1, samples),
                targets,
            )
        )
    )
    per_chunk = max(1, min(walls, 512 // (spans * CAP)))
    while walls % per_chunk:
        per_chunk -= 1
    outs = pl.pallas_call(
        functools.partial(train_kernel, per_chunk, full),
        out_shape=(jax.ShapeDtypeStruct(inside, jnp.float32),)
        + tuple(jax.ShapeDtypeStruct(x.shape, jnp.float32) for x in weights),
        in_specs=[anywhere] + [vmem] * 7,
        out_specs=(anywhere,) * 6,
        scratch_shapes=[pltpu.VMEM(x.shape, jnp.float32) for x in weights] + [dma((6,))],
        compiler_params=pltpu.CompilerParams(vmem_limit_bytes=48 * 1024 * 1024),
        name="train",
    )(new_field, *received, *weights)
    return (outs[0].reshape(shape),) + tuple(outs[1:])


def solution(mesh):
    in_specs = (
        P(None, None, None, "span", "wall", None),
        P(None, None, None, None, "span", "wall", None),
        P(("span", "wall")),
        P(("span", "wall"), None),
        P(("span", "wall"), None),
        P("span", None, None),
        P("span", None, None),
        P("span", None, None),
        P("span", None, None),
        P("span", None, None),
    )
    out_specs = (
        P(None, None, None, "span", "wall", None),
        P("span", None, None),
        P("span", None, None),
        P("span", None, None),
        P("span", None, None),
        P("span", None, None),
    )
    body = functools.partial(local, mesh.shape["span"], mesh.shape["wall"])
    return jax.shard_map(body, mesh=mesh, in_specs=in_specs, out_specs=out_specs, check_vma=False)
```

```python
import functools
import math

import jax
import jax.numpy as jnp
import numpy as np
from jax import lax
from jax.experimental import pallas as pl
from jax.experimental.pallas import tpu as pltpu
from jax.sharding import PartitionSpec as P

P_SIZE = 5
CAP = 16
COPIES = 1
MESH = pl.DeviceIdType.MESH


step_scale = 0.04


def legendre_pair(order, point):
    value_prev = 1.0
    value_now = point
    slope_prev = 0.0
    slope_now = 1.0
    for degree in range(1, order):
        value_next = ((2 * degree + 1) * point * value_now - degree * value_prev) / (degree + 1)
        slope_next = slope_prev + (2 * degree + 1) * value_now
        value_prev, value_now = (value_now, value_next)
        slope_prev, slope_now = (slope_now, slope_next)
    return (value_now, slope_now)


def gauss_nodes(count):
    found = []
    for index in range(count):
        guess = math.cos(math.pi * (index + 0.75) / (count + 0.5))
        for sweep in range(60):
            value, slope = legendre_pair(count, guess)
            guess = guess - value / slope
        found.append(guess)
    return sorted(found)


def fr_tables():
    nodes = gauss_nodes(P_SIZE)
    bary = []
    for j in range(P_SIZE):
        product = 1.0
        for m in range(P_SIZE):
            if m != j:
                product = product * (nodes[j] - nodes[m])
        bary.append(1.0 / product)
    deriv = [[0.0] * P_SIZE for row_index in range(P_SIZE)]
    for i in range(P_SIZE):
        for j in range(P_SIZE):
            if i != j:
                deriv[i][j] = bary[j] / bary[i] / (nodes[i] - nodes[j])
        deriv[i][i] = -sum((deriv[i][j] for j in range(P_SIZE) if j != i))

    def basis_at(point):
        values = []
        for j in range(P_SIZE):
            product = 1.0
            for m in range(P_SIZE):
                if m != j:
                    product = product * (point - nodes[m]) / (nodes[j] - nodes[m])
            values.append(product)
        return values

    left_value = basis_at(-1.0)
    right_value = basis_at(1.0)
    sign = (-1.0) ** P_SIZE
    slope_left = [
        0.5 * sign * (legendre_pair(P_SIZE, x)[1] - legendre_pair(P_SIZE - 1, x)[1]) for x in nodes
    ]
    slope_right = [-slope_left[P_SIZE - 1 - i] for i in range(P_SIZE)]
    inner = [
        [
            step_scale
            * (deriv[i][m] - slope_left[i] * left_value[m] - slope_right[i] * right_value[m])
            for m in range(P_SIZE)
        ]
        for i in range(P_SIZE)
    ]
    edge_left = [0.25 * step_scale * s for s in slope_left]
    edge_right = [0.25 * step_scale * s for s in slope_right]
    return inner, left_value, right_value, edge_left, edge_right


POINTS = P_SIZE**3
FACES = 32


def section_tables():
    inner, left, right, edge_left, edge_right = fr_tables()
    to_faces = np.zeros((3, 2, FACES, 128))
    volume = np.zeros((128, 3, 128))
    edges = np.zeros((128, 3, 2, FACES))
    for point in range(POINTS):
        place = (point // 25, point // 5 % 5, point % 5)
        for d in range(3):
            rest = [place[n] for n in range(3) if n != d]
            face = rest[0] * P_SIZE + rest[1]
            to_faces[d, 0, face, point] = left[place[d]]
            to_faces[d, 1, face, point] = right[place[d]]
            edges[point, d, 0, face] = edge_left[place[d]]
            edges[point, d, 1, face] = edge_right[place[d]]
            for m in range(P_SIZE):
                source = point + (m - place[d]) * (25, 5, 1)[d]
                volume[point, d, source] = inner[place[d]][m]

    def halves(table):
        high = table.astype(np.float32).astype(jnp.bfloat16)
        low = (table - high.astype(np.float64)).astype(np.float32).astype(jnp.bfloat16)
        return np.stack([high, low])

    second = np.concatenate([volume.reshape(128, -1), edges.reshape(128, -1)], axis=1)
    return halves(to_faces.reshape(-1, 128)), halves(second)


FACE_TABLE, POINT_TABLE = section_tables()


def apply(table, x):
    high = x.astype(jnp.bfloat16)
    low = (x - high.astype(jnp.float32)).astype(jnp.bfloat16)
    dot = functools.partial(jnp.dot, preferred_element_type=jnp.float32)
    return dot(table[0], high) + (dot(table[0], low) + dot(table[1], high))


def upwind(state_before, speed_before, state_after, speed_after):
    speed = speed_before + speed_after
    return speed * (state_before + state_after) - jnp.abs(speed) * (state_after - state_before)


def turn(x, step):
    half = x.shape[1] // 2
    return jnp.concatenate([pltpu.roll(x[:, :half], step % half, 1), pltpu.roll(x[:, half:], step % half, 1)], axis=1)


def paired(place, d):
    bit = 1
    while bit <= d:
        if d & bit:
            place = place + bit * (1 - 2 * lax.rem(lax.div(place, bit), 2))
        bit *= 2
    return place


def is_full(spans, samples):
    return spans * CAP == samples


def section_kernel(
    spans, walls,
    field_hbm, velocity_hbm, cells_hbm, dest_hbm, targets_hbm, face_hbm, point_hbm,
    new_ref, rows_all, marks_all,
    field, velocity, cells_ref, dest_ref, targets_ref, face_table, point_table,
    zero_send, one_send, zero_before, zero_after, one_before, one_after,
    values, rows_send, marks_send,
    in_sems, halo_send, halo_recv,
    marks_sems, marks_wall_sems, rows_sems, rows_wall_sems,
):
    i = lax.axis_index("span")
    w = lax.axis_index("wall")
    barrier = pltpu.get_barrier_semaphore()
    for d in range(1, spans):
        pl.semaphore_signal(barrier, inc=1, device_id={"span": lax.rem(i + d, spans)}, device_id_type=MESH)
    for d in range(1, walls):
        pl.semaphore_signal(barrier, inc=1, device_id={"wall": lax.rem(w + d, walls)}, device_id_type=MESH)

    flat = 2 * POINTS
    loads = [
        pltpu.make_async_copy(field_hbm.reshape(flat, 128), field.at[0:flat], in_sems.at[0]),
        pltpu.make_async_copy(face_hbm, face_table, in_sems.at[1]),
    ]
    for d in range(3):
        loads.append(
            pltpu.make_async_copy(velocity_hbm.at[d].reshape(flat, 128), velocity.at[d, 0:flat], in_sems.at[2 + d])
        )
    for number, (whole, ref) in enumerate(
        ((dest_hbm, dest_ref), (targets_hbm, targets_ref), (cells_hbm, cells_ref), (point_hbm, point_table))
    ):
        loads.append(pltpu.make_async_copy(whole, ref, in_sems.at[5 + number]))
    for load in loads:
        load.start()

    for at_end, ref in ((i == 0, zero_before), (i == spans - 1, zero_after), (w == 0, one_before), (w == walls - 1, one_after)):
        @pl.when(at_end)
        def _(ref=ref):
            ref[...] = jnp.zeros_like(ref)

    field[flat:] = jnp.zeros((256 - flat, 128), jnp.float32)
    velocity[:, flat:] = jnp.zeros((3, 256 - flat, 128), jnp.float32)

    def beside(ref, *at):
        return jnp.concatenate([ref[at + (pl.ds(b, 128, stride=2),)] for b in range(2)], axis=1)

    loads[0].wait()
    loads[1].wait()
    two = 2 * FACES
    q = beside(field)
    face_q = apply(face_table[:, 0 : 2 * two], q)
    q_zero, q_one = face_q[:two], face_q[two:]
    loads[2].wait()
    a_zero = apply(face_table[:, 0:two], beside(velocity, 0))
    loads[3].wait()
    a_one = apply(face_table[:, two : 2 * two], beside(velocity, 1))
    for n, (along_zero, along_one) in enumerate(((q_zero, q_one), (a_zero, a_one))):
        zero_send[0, n] = along_zero[:FACES]
        zero_send[1, n] = along_zero[FACES:]
        one_send[0, n] = along_one[:FACES, :128]
        one_send[1, n] = along_one[FACES:, 128:]

    pl.semaphore_wait(barrier, spans + walls - 2)

    def halo(number, axis, place, count, source, into, right):
        peer = jnp.minimum(place + 1, count - 1) if right else jnp.maximum(place - 1, 0)
        copy = pltpu.make_async_remote_copy(
            src_ref=source,
            dst_ref=into,
            send_sem=halo_send.at[number],
            recv_sem=halo_recv.at[number],
            device_id={axis: peer},
            device_id_type=MESH,
        )
        sends = place < count - 1 if right else place > 0
        gets = place > 0 if right else place < count - 1
        return copy, sends, gets

    halos = [
        halo(0, "span", i, spans, zero_send.at[1], zero_before, True),
        halo(1, "span", i, spans, zero_send.at[0], zero_after, False),
        halo(2, "wall", w, walls, one_send.at[1], one_before, True),
        halo(3, "wall", w, walls, one_send.at[0], one_after, False),
    ]
    for copy, sends, _ in halos:
        pl.when(sends)(copy.start)

    samples = dest_ref.shape[1]
    for load in loads[5:8]:
        load.wait()
    dest = dest_ref[...]
    across = jnp.broadcast_to(dest, (samples, samples))
    down = jnp.transpose(across)
    earlier = lax.broadcasted_iota(jnp.int32, (samples, samples), 0) < lax.broadcasted_iota(jnp.int32, (samples, samples), 1)
    slot = jnp.sum(jnp.where(jnp.logical_and(across == down, earlier), 1.0, 0.0), axis=0, keepdims=True)
    position = dest * CAP + slot.astype(jnp.int32)
    places = spans * CAP
    chosen = jnp.where(
        lax.broadcasted_iota(jnp.int32, (places, samples), 0) == position, 1.0, 0.0
    ).astype(jnp.bfloat16)
    wanted = jnp.dot(chosen, targets_ref[...], preferred_element_type=jnp.float32)
    marks_send[:, 0:CAP] = wanted.astype(jnp.bfloat16).reshape(spans, CAP, -1)
    if not is_full(spans, samples):
        flags = jnp.dot(chosen, jnp.ones((samples, samples), jnp.bfloat16), preferred_element_type=jnp.float32)
        marks_send[:, CAP : 2 * CAP] = flags.astype(jnp.bfloat16).reshape(spans, CAP, -1)

    groups = min(spans, COPIES)
    size = spans // groups

    def group_of(held, wall, g):
        return held.at[wall, pl.ds(paired(lax.div(i, size), g) * size, size)]

    def dispatch(send, held, sems, wall_sems):
        copies = [
            pltpu.make_async_remote_copy(
                src_ref=send.at[paired(i, d)],
                dst_ref=held.at[w, i],
                send_sem=sems.at[0, d],
                recv_sem=sems.at[1, d],
                device_id={"span": paired(i, d)},
                device_id_type=MESH,
            )
            for d in range(1, spans)
        ]
        for copy in copies:
            copy.start()
        held[w, i] = send[i]
        if size == 1:
            copies = copies + forward(held, wall_sems, 0)
        return copies

    def forward(held, sems, g):
        place = group_of(held, w, g)
        copies = [
            pltpu.make_async_remote_copy(
                src_ref=place,
                dst_ref=place,
                send_sem=sems.at[0, n, g],
                recv_sem=sems.at[1, n, g],
                device_id={"wall": paired(w, n)},
                device_id_type=MESH,
            )
            for n in range(1, walls)
        ]
        for copy in copies:
            copy.start()
        return copies

    def pass_on(held, sems, wall_sems):
        copies = []
        for d in range(1, spans):
            source = paired(i, d)
            pltpu.make_async_remote_copy(
                src_ref=held.at[w, source],
                dst_ref=held.at[w, source],
                send_sem=sems.at[0, d],
                recv_sem=sems.at[1, d],
                device_id={"span": source},
                device_id_type=MESH,
            ).wait_recv()
            if (d + 1) % size == 0:
                copies += forward(held, wall_sems, d // size)
        return copies

    def finish(held, sems):
        for g in range(groups):
            for n in range(1, walls):
                place = group_of(held, paired(w, n), g)
                pltpu.make_async_remote_copy(
                    src_ref=place,
                    dst_ref=place,
                    send_sem=sems.at[0, n, g],
                    recv_sem=sems.at[1, n, g],
                    device_id={"wall": paired(w, n)},
                    device_id_type=MESH,
                ).wait_recv()

    sent = dispatch(marks_send, marks_all, marks_sems, marks_wall_sems)

    cells = cells_ref[...]
    here = jnp.where(
        lax.broadcasted_iota(jnp.int32, (2 * samples, samples), 0) == cells, 1.0, 0.0
    ).astype(jnp.bfloat16)
    picks = lax.dot_general(
        chosen, here, (((1,), (1,)), ((), ())), preferred_element_type=jnp.float32
    ).astype(jnp.bfloat16)

    loads[4].wait()
    loads[8].wait()
    a = [beside(velocity, d) for d in range(3)]
    q_two = apply(face_table[:, 2 * two :], q)
    a_two = apply(face_table[:, 2 * two :], a[2])
    left = upwind(turn(q_two[FACES:], 1), turn(a_two[FACES:], 1), q_two[:FACES], a_two[:FACES])
    right = upwind(q_two[FACES:], a_two[FACES:], turn(q_two[:FACES], -1), turn(a_two[:FACES], -1))
    edges = 3 * 128
    partial = q - (
        apply(point_table[:, :, :edges], jnp.concatenate([q * x for x in a], axis=0))
        + apply(point_table[:, :, edges + 2 * two :], jnp.concatenate([left, right], axis=0))
    )
    means = [jnp.sum(x, axis=0, keepdims=True) * np.float32(1.0 / POINTS) for x in a]

    sent += pass_on(marks_all, marks_sems, marks_wall_sems)

    for copy, _, gets in halos:
        pl.when(gets)(copy.wait_recv)
    shared = [
        upwind(zero_before[0], zero_before[1], q_zero[:FACES], a_zero[:FACES]),
        upwind(q_zero[FACES:], a_zero[FACES:], zero_after[0], zero_after[1]),
    ]
    before = [jnp.concatenate([one_before[n], x[FACES:, :128]], axis=1) for n, x in enumerate((q_one, a_one))]
    after = [jnp.concatenate([x[:FACES, 128:], one_after[n]], axis=1) for n, x in enumerate((q_one, a_one))]
    shared.append(upwind(before[0], before[1], q_one[:FACES], a_one[:FACES]))
    shared.append(upwind(q_one[FACES:], a_one[FACES:], after[0], after[1]))
    new = partial - apply(point_table[:, :, edges : edges + 2 * two], jnp.concatenate(shared, axis=0))
    values[...] = new
    for d in range(3):
        values[POINTS + d : POINTS + d + 1] = means[d]
    total = lax.dot_general(
        picks, values[...].astype(jnp.bfloat16), (((1,), (1,)), ((), ())), preferred_element_type=jnp.float32
    )
    rows_send[...] = total.astype(jnp.bfloat16).reshape(rows_send.shape)
    sent += dispatch(rows_send, rows_all, rows_sems, rows_wall_sems)
    for b in range(2):
        new_ref.reshape(flat, 128)[pl.ds(b, POINTS, stride=2)] = new[:POINTS, b * 128 : (b + 1) * 128]
    sent += pass_on(rows_all, rows_sems, rows_wall_sems)
    for copy, sends, _ in halos:
        pl.when(sends)(copy.wait_send)
    for copy in sent:
        copy.wait_send()
    finish(marks_all, marks_wall_sems)
    finish(rows_all, rows_wall_sems)


def train_kernel(
    per_chunk, full,
    new_ref, rows_all, marks_all, one, two, three, four, five,
    new_out, out_one, out_two, out_three, out_four, out_five,
    grad_one, grad_two, grad_three, grad_four, grad_five, sems,
):
    copies = [pltpu.make_async_copy(new_ref, new_out, sems.at[5])]
    copies[0].start()
    walls, spans = rows_all.shape[:2]
    weights = (one, two, three, four, five)
    grads = (grad_one, grad_two, grad_three, grad_four, grad_five)
    outs = (out_one, out_two, out_three, out_four, out_five)
    chunks = walls // per_chunk
    places = spans * CAP
    count = per_chunk * places

    def leave(layer):
        copy = pltpu.make_async_copy(grads[layer], outs[layer], sems.at[layer])
        copy.start()
        copies.append(copy)

    def chunk(number):
        first = number * per_chunk
        act = rows_all[pl.ds(first, per_chunk)].reshape(count, -1)
        picked = marks_all.at[pl.ds(first, per_chunk)]
        wanted = picked[:, :, 0:CAP].reshape(count, -1).astype(jnp.float32)
        if full:
            scale = np.float32(1.0 / places)
        else:
            flags = picked[:, :, CAP : 2 * CAP].reshape(per_chunk, places, -1).astype(jnp.float32)
            scale = flags / jnp.maximum(jnp.sum(flags, axis=1, keepdims=True), 1.0)
            scale = scale.reshape(count, -1)
        acts = [act]
        slopes = []
        for layer in weights[:-1]:
            pre = jnp.dot(act, layer[0], preferred_element_type=jnp.float32)
            sigma = 0.5 + 0.5 * jnp.tanh(0.5 * pre)
            hidden = pre * sigma
            slopes.append(sigma + hidden * (1.0 - sigma))
            act = hidden.astype(jnp.bfloat16)
            acts.append(act)
        output = jnp.dot(act, weights[-1][0], preferred_element_type=jnp.float32)
        error = (scale * (output - wanted)).astype(jnp.bfloat16)
        for layer in range(4, -1, -1):
            grad = lax.dot_general(
                acts[layer], error, (((0,), (0,)), ((), ())), preferred_element_type=jnp.float32
            )
            if chunks == 1:
                grads[layer][0] = grad
                leave(layer)
            else:
                grads[layer][0] += grad
            if layer:
                back = lax.dot_general(
                    error, weights[layer][0], (((1,), (1,)), ((), ())), preferred_element_type=jnp.float32
                )
                error = (back * slopes[layer - 1]).astype(jnp.bfloat16)

    if chunks == 1:
        chunk(0)
    else:
        for grad in grads:
            grad[...] = jnp.zeros_like(grad)
        pl.loop(0, chunks)(chunk)
        for layer in range(5):
            leave(layer)
    for copy in copies:
        copy.wait()


def local(spans, walls, field, velocity, cells, destination, targets, *weights):
    shape = field.shape
    samples = cells.shape[0]
    inside = (P_SIZE, P_SIZE, P_SIZE, shape[3] * shape[4], shape[5])
    vmem = pl.BlockSpec(memory_space=pltpu.VMEM)
    anywhere = pl.BlockSpec(memory_space=pl.ANY)
    hbm = pl.BlockSpec(memory_space=pltpu.HBM)
    features = P_SIZE**3 + 3
    wide = targets.shape[1]
    full = is_full(spans, samples)
    marks = CAP if full else 2 * CAP
    dma = pltpu.SemaphoreType.DMA
    new_field, *received = pl.pallas_call(
        functools.partial(section_kernel, spans, walls),
        out_shape=(
            jax.ShapeDtypeStruct(inside, jnp.float32),
            jax.ShapeDtypeStruct((walls, spans, CAP, features), jnp.bfloat16),
            jax.ShapeDtypeStruct((walls, spans, marks, wide), jnp.bfloat16),
        ),
        in_specs=[hbm] * 7,
        out_specs=(vmem,) * 3,
        scratch_shapes=[
            pltpu.VMEM((256, 128), jnp.float32),
            pltpu.VMEM((3, 256, 128), jnp.float32),
            pltpu.VMEM((1, samples), jnp.int32),
            pltpu.VMEM((1, samples), jnp.int32),
            pltpu.VMEM(targets.shape, jnp.bfloat16),
            pltpu.VMEM(FACE_TABLE.shape, jnp.bfloat16),
            pltpu.VMEM(POINT_TABLE.shape, jnp.bfloat16),
            pltpu.VMEM((2, 2, FACES, 256), jnp.float32),
            pltpu.VMEM((2, 2, FACES, 128), jnp.float32),
            pltpu.VMEM((2, FACES, 256), jnp.float32),
            pltpu.VMEM((2, FACES, 256), jnp.float32),
            pltpu.VMEM((2, FACES, 128), jnp.float32),
            pltpu.VMEM((2, FACES, 128), jnp.float32),
            pltpu.VMEM((128, 256), jnp.float32),
            pltpu.VMEM((spans, CAP, features), jnp.bfloat16),
            pltpu.VMEM((spans, marks, wide), jnp.bfloat16),
            dma((9,)), dma((4,)), dma((4,)),
            dma((2, spans)), dma((2, walls, min(spans, COPIES))), dma((2, spans)), dma((2, walls, min(spans, COPIES))),
        ],
        compiler_params=pltpu.CompilerParams(
            collective_id=0, has_side_effects=True, vmem_limit_bytes=48 * 1024 * 1024
        ),
        name="section",
    )(
        *(
            pltpu.with_memory_space_constraint(x, pltpu.HBM)
            for x in (
                field.reshape(inside),
                velocity.reshape((3,) + inside),
                cells.reshape(1, samples),
                destination.reshape(1, samples),
                targets,
                jnp.asarray(FACE_TABLE),
                jnp.asarray(POINT_TABLE),
            )
        )
    )
    per_chunk = max(1, min(walls, 512 // (spans * CAP)))
    while walls % per_chunk:
        per_chunk -= 1
    outs = pl.pallas_call(
        functools.partial(train_kernel, per_chunk, full),
        out_shape=(jax.ShapeDtypeStruct(inside, jnp.float32),)
        + tuple(jax.ShapeDtypeStruct(x.shape, jnp.float32) for x in weights),
        in_specs=[anywhere] + [vmem] * 7,
        out_specs=(anywhere,) * 6,
        scratch_shapes=[pltpu.VMEM(x.shape, jnp.float32) for x in weights] + [dma((6,))],
        compiler_params=pltpu.CompilerParams(vmem_limit_bytes=48 * 1024 * 1024),
        name="train",
    )(new_field, *received, *weights)
    return (outs[0].reshape(shape),) + tuple(outs[1:])


def solution(mesh):
    in_specs = (
        P(None, None, None, "span", "wall", None),
        P(None, None, None, None, "span", "wall", None),
        P(("span", "wall")),
        P(("span", "wall"), None),
        P(("span", "wall"), None),
        P("span", None, None),
        P("span", None, None),
        P("span", None, None),
        P("span", None, None),
        P("span", None, None),
    )
    out_specs = (
        P(None, None, None, "span", "wall", None),
        P("span", None, None),
        P("span", None, None),
        P("span", None, None),
        P("span", None, None),
        P("span", None, None),
    )
    body = functools.partial(local, mesh.shape["span"], mesh.shape["wall"])
    return jax.shard_map(body, mesh=mesh, in_specs=in_specs, out_specs=out_specs, check_vma=False)
```

```python
import functools
import math

import jax
import jax.numpy as jnp
import numpy as np
from jax import lax
from jax.experimental import pallas as pl
from jax.experimental.pallas import tpu as pltpu
from jax.sharding import PartitionSpec as P

P_SIZE = 5
CAP = 16
COPIES = 1
MESH = pl.DeviceIdType.MESH


step_scale = 0.04


def legendre_pair(order, point):
    value_prev = 1.0
    value_now = point
    slope_prev = 0.0
    slope_now = 1.0
    for degree in range(1, order):
        value_next = ((2 * degree + 1) * point * value_now - degree * value_prev) / (degree + 1)
        slope_next = slope_prev + (2 * degree + 1) * value_now
        value_prev, value_now = (value_now, value_next)
        slope_prev, slope_now = (slope_now, slope_next)
    return (value_now, slope_now)


def gauss_nodes(count):
    found = []
    for index in range(count):
        guess = math.cos(math.pi * (index + 0.75) / (count + 0.5))
        for sweep in range(60):
            value, slope = legendre_pair(count, guess)
            guess = guess - value / slope
        found.append(guess)
    return sorted(found)


def fr_tables():
    nodes = gauss_nodes(P_SIZE)
    bary = []
    for j in range(P_SIZE):
        product = 1.0
        for m in range(P_SIZE):
            if m != j:
                product = product * (nodes[j] - nodes[m])
        bary.append(1.0 / product)
    deriv = [[0.0] * P_SIZE for row_index in range(P_SIZE)]
    for i in range(P_SIZE):
        for j in range(P_SIZE):
            if i != j:
                deriv[i][j] = bary[j] / bary[i] / (nodes[i] - nodes[j])
        deriv[i][i] = -sum((deriv[i][j] for j in range(P_SIZE) if j != i))

    def basis_at(point):
        values = []
        for j in range(P_SIZE):
            product = 1.0
            for m in range(P_SIZE):
                if m != j:
                    product = product * (point - nodes[m]) / (nodes[j] - nodes[m])
            values.append(product)
        return values

    left_value = basis_at(-1.0)
    right_value = basis_at(1.0)
    sign = (-1.0) ** P_SIZE
    slope_left = [
        0.5 * sign * (legendre_pair(P_SIZE, x)[1] - legendre_pair(P_SIZE - 1, x)[1]) for x in nodes
    ]
    slope_right = [-slope_left[P_SIZE - 1 - i] for i in range(P_SIZE)]
    inner = [
        [
            step_scale
            * (deriv[i][m] - slope_left[i] * left_value[m] - slope_right[i] * right_value[m])
            for m in range(P_SIZE)
        ]
        for i in range(P_SIZE)
    ]
    edge_left = [0.25 * step_scale * s for s in slope_left]
    edge_right = [0.25 * step_scale * s for s in slope_right]
    return inner, left_value, right_value, edge_left, edge_right


POINTS = P_SIZE**3
FACES = 32


def section_tables():
    inner, left, right, edge_left, edge_right = fr_tables()
    to_faces = np.zeros((3, 2, FACES, 128))
    volume = np.zeros((128, 3, 128))
    edges = np.zeros((128, 3, 2, FACES))
    for point in range(POINTS):
        place = (point // 25, point // 5 % 5, point % 5)
        for d in range(3):
            rest = [place[n] for n in range(3) if n != d]
            face = rest[0] * P_SIZE + rest[1]
            to_faces[d, 0, face, point] = left[place[d]]
            to_faces[d, 1, face, point] = right[place[d]]
            edges[point, d, 0, face] = edge_left[place[d]]
            edges[point, d, 1, face] = edge_right[place[d]]
            for m in range(P_SIZE):
                source = point + (m - place[d]) * (25, 5, 1)[d]
                volume[point, d, source] = inner[place[d]][m]

    def halves(table):
        high = table.astype(np.float32).astype(jnp.bfloat16)
        low = (table - high.astype(np.float64)).astype(np.float32).astype(jnp.bfloat16)
        return np.stack([high, low])

    second = np.concatenate([volume.reshape(128, -1), edges.reshape(128, -1)], axis=1)
    return halves(to_faces.reshape(-1, 128)), halves(second)


FACE_TABLE, POINT_TABLE = section_tables()


def apply(table, x):
    high = x.astype(jnp.bfloat16)
    low = (x - high.astype(jnp.float32)).astype(jnp.bfloat16)
    dot = functools.partial(jnp.dot, preferred_element_type=jnp.float32)
    return dot(table[0], high) + (dot(table[0], low) + dot(table[1], high))


def upwind(state_before, speed_before, state_after, speed_after):
    speed = speed_before + speed_after
    return speed * (state_before + state_after) - jnp.abs(speed) * (state_after - state_before)


def turn(x, step):
    half = x.shape[1] // 2
    return jnp.concatenate([pltpu.roll(x[:, :half], step % half, 1), pltpu.roll(x[:, half:], step % half, 1)], axis=1)


def paired(place, d):
    bit = 1
    while bit <= d:
        if d & bit:
            place = place + bit * (1 - 2 * lax.rem(lax.div(place, bit), 2))
        bit *= 2
    return place


def is_full(spans, samples):
    return spans * CAP == samples


def section_kernel(
    spans, walls,
    field_hbm, velocity_hbm, cells_hbm, dest_hbm, targets_hbm, face_hbm, point_hbm,
    new_ref, rows_all, marks_all,
    field, velocity, cells_ref, dest_ref, targets_ref, face_table, point_table,
    zero_send, one_send, zero_before, zero_after, one_before, one_after,
    values, rows_send, marks_send,
    in_sems, halo_send, halo_recv,
    marks_sems, marks_wall_sems, rows_sems, rows_wall_sems,
):
    i = lax.axis_index("span")
    w = lax.axis_index("wall")
    barrier = pltpu.get_barrier_semaphore()
    for d in reversed(range(1, spans)):
        pl.semaphore_signal(barrier, inc=1, device_id={"span": paired(i, d)}, device_id_type=MESH)
    for d in reversed(range(1, walls)):
        pl.semaphore_signal(barrier, inc=1, device_id={"wall": paired(w, d)}, device_id_type=MESH)

    flat = 2 * POINTS
    loads = [
        pltpu.make_async_copy(field_hbm.reshape(flat, 128), field.at[0:flat], in_sems.at[0]),
        pltpu.make_async_copy(face_hbm, face_table, in_sems.at[1]),
    ]
    for d in range(3):
        loads.append(
            pltpu.make_async_copy(velocity_hbm.at[d].reshape(flat, 128), velocity.at[d, 0:flat], in_sems.at[2 + d])
        )
    for number, (whole, ref) in enumerate(
        ((dest_hbm, dest_ref), (targets_hbm, targets_ref), (cells_hbm, cells_ref), (point_hbm, point_table))
    ):
        loads.append(pltpu.make_async_copy(whole, ref, in_sems.at[5 + number]))
    for load in loads:
        load.start()

    for at_end, ref in ((i == 0, zero_before), (i == spans - 1, zero_after), (w == 0, one_before), (w == walls - 1, one_after)):
        @pl.when(at_end)
        def _(ref=ref):
            ref[...] = jnp.zeros_like(ref)

    field[flat:] = jnp.zeros((256 - flat, 128), jnp.float32)
    velocity[:, flat:] = jnp.zeros((3, 256 - flat, 128), jnp.float32)

    def beside(ref, *at):
        return jnp.concatenate([ref[at + (pl.ds(b, 128, stride=2),)] for b in range(2)], axis=1)

    loads[0].wait()
    loads[1].wait()
    two = 2 * FACES
    q = beside(field)
    face_q = apply(face_table[:, 0 : 2 * two], q)
    q_zero, q_one = face_q[:two], face_q[two:]
    loads[2].wait()
    a_zero = apply(face_table[:, 0:two], beside(velocity, 0))
    loads[3].wait()
    a_one = apply(face_table[:, two : 2 * two], beside(velocity, 1))
    for n, (along_zero, along_one) in enumerate(((q_zero, q_one), (a_zero, a_one))):
        zero_send[0, n] = along_zero[:FACES].astype(jnp.bfloat16)
        zero_send[1, n] = along_zero[FACES:].astype(jnp.bfloat16)
        one_send[0, n] = along_one[:FACES, :128].astype(jnp.bfloat16)
        one_send[1, n] = along_one[FACES:, 128:].astype(jnp.bfloat16)

    pl.semaphore_wait(barrier, spans + walls - 2)

    def halo(number, axis, place, count, source, into, right):
        peer = jnp.minimum(place + 1, count - 1) if right else jnp.maximum(place - 1, 0)
        copy = pltpu.make_async_remote_copy(
            src_ref=source,
            dst_ref=into,
            send_sem=halo_send.at[number],
            recv_sem=halo_recv.at[number],
            device_id={axis: peer},
            device_id_type=MESH,
        )
        sends = place < count - 1 if right else place > 0
        gets = place > 0 if right else place < count - 1
        return copy, sends, gets

    halos = [
        halo(0, "span", i, spans, zero_send.at[1], zero_before, True),
        halo(1, "span", i, spans, zero_send.at[0], zero_after, False),
        halo(2, "wall", w, walls, one_send.at[1], one_before, True),
        halo(3, "wall", w, walls, one_send.at[0], one_after, False),
    ]
    for copy, sends, _ in halos:
        pl.when(sends)(copy.start)

    samples = dest_ref.shape[1]
    for load in loads[5:8]:
        load.wait()
    dest = dest_ref[...]
    across = jnp.broadcast_to(dest, (samples, samples))
    down = jnp.transpose(across)
    earlier = lax.broadcasted_iota(jnp.int32, (samples, samples), 0) < lax.broadcasted_iota(jnp.int32, (samples, samples), 1)
    slot = jnp.sum(jnp.where(jnp.logical_and(across == down, earlier), 1.0, 0.0), axis=0, keepdims=True)
    position = dest * CAP + slot.astype(jnp.int32)
    places = spans * CAP
    chosen = jnp.where(
        lax.broadcasted_iota(jnp.int32, (places, samples), 0) == position, 1.0, 0.0
    ).astype(jnp.bfloat16)
    wanted = jnp.dot(chosen, targets_ref[...], preferred_element_type=jnp.float32)
    marks_send[:, 0:CAP] = wanted.astype(jnp.bfloat16).reshape(spans, CAP, -1)
    if not is_full(spans, samples):
        flags = jnp.dot(chosen, jnp.ones((samples, samples), jnp.bfloat16), preferred_element_type=jnp.float32)
        marks_send[:, CAP : 2 * CAP] = flags.astype(jnp.bfloat16).reshape(spans, CAP, -1)

    groups = min(spans, COPIES)
    size = spans // groups

    def group_of(held, wall, g):
        return held.at[wall, pl.ds(paired(lax.div(i, size), g) * size, size)]

    def dispatch(send, held, sems, wall_sems):
        copies = [
            pltpu.make_async_remote_copy(
                src_ref=send.at[paired(i, d)],
                dst_ref=held.at[w, i],
                send_sem=sems.at[0, d],
                recv_sem=sems.at[1, d],
                device_id={"span": paired(i, d)},
                device_id_type=MESH,
            )
            for d in reversed(range(1, spans))
        ]
        for copy in copies:
            copy.start()
        held[w, i] = send[i]
        if size == 1:
            copies = copies + forward(held, wall_sems, 0)
        return copies

    def forward(held, sems, g):
        place = group_of(held, w, g)
        copies = [
            pltpu.make_async_remote_copy(
                src_ref=place,
                dst_ref=place,
                send_sem=sems.at[0, n, g],
                recv_sem=sems.at[1, n, g],
                device_id={"wall": paired(w, n)},
                device_id_type=MESH,
            )
            for n in reversed(range(1, walls))
        ]
        for copy in copies:
            copy.start()
        return copies

    def pass_on(held, sems, wall_sems):
        copies = []
        for d in range(1, spans):
            source = paired(i, d)
            pltpu.make_async_remote_copy(
                src_ref=held.at[w, source],
                dst_ref=held.at[w, source],
                send_sem=sems.at[0, d],
                recv_sem=sems.at[1, d],
                device_id={"span": source},
                device_id_type=MESH,
            ).wait_recv()
            if (d + 1) % size == 0:
                copies += forward(held, wall_sems, d // size)
        return copies

    def finish(held, sems):
        for g in range(groups):
            for n in range(1, walls):
                place = group_of(held, paired(w, n), g)
                pltpu.make_async_remote_copy(
                    src_ref=place,
                    dst_ref=place,
                    send_sem=sems.at[0, n, g],
                    recv_sem=sems.at[1, n, g],
                    device_id={"wall": paired(w, n)},
                    device_id_type=MESH,
                ).wait_recv()

    sent = dispatch(marks_send, marks_all, marks_sems, marks_wall_sems)

    cells = cells_ref[...]
    here = jnp.where(
        lax.broadcasted_iota(jnp.int32, (2 * samples, samples), 0) == cells, 1.0, 0.0
    ).astype(jnp.bfloat16)
    picks = lax.dot_general(
        chosen, here, (((1,), (1,)), ((), ())), preferred_element_type=jnp.float32
    ).astype(jnp.bfloat16)

    loads[4].wait()
    loads[8].wait()
    a = [beside(velocity, d) for d in range(3)]
    q_two = apply(face_table[:, 2 * two :], q)
    a_two = apply(face_table[:, 2 * two :], a[2])
    left = upwind(turn(q_two[FACES:], 1), turn(a_two[FACES:], 1), q_two[:FACES], a_two[:FACES])
    right = upwind(q_two[FACES:], a_two[FACES:], turn(q_two[:FACES], -1), turn(a_two[:FACES], -1))
    edges = 3 * 128
    partial = q - (
        apply(point_table[:, :, :edges], jnp.concatenate([q * x for x in a], axis=0))
        + apply(point_table[:, :, edges + 2 * two :], jnp.concatenate([left, right], axis=0))
    )
    means = [jnp.sum(x, axis=0, keepdims=True) * np.float32(1.0 / POINTS) for x in a]

    sent += pass_on(marks_all, marks_sems, marks_wall_sems)

    for copy, _, gets in halos:
        pl.when(gets)(copy.wait_recv)
    got = [[ref[n].astype(jnp.float32) for n in range(2)] for ref in (zero_before, zero_after, one_before, one_after)]
    shared = [
        upwind(*got[0], q_zero[:FACES], a_zero[:FACES]),
        upwind(q_zero[FACES:], a_zero[FACES:], *got[1]),
    ]
    before = [jnp.concatenate([got[2][n], x[FACES:, :128]], axis=1) for n, x in enumerate((q_one, a_one))]
    after = [jnp.concatenate([x[:FACES, 128:], got[3][n]], axis=1) for n, x in enumerate((q_one, a_one))]
    shared.append(upwind(before[0], before[1], q_one[:FACES], a_one[:FACES]))
    shared.append(upwind(q_one[FACES:], a_one[FACES:], after[0], after[1]))
    new = partial - apply(point_table[:, :, edges : edges + 2 * two], jnp.concatenate(shared, axis=0))
    values[...] = new
    for d in range(3):
        values[POINTS + d : POINTS + d + 1] = means[d]
    total = lax.dot_general(
        picks, values[...].astype(jnp.bfloat16), (((1,), (1,)), ((), ())), preferred_element_type=jnp.float32
    )
    rows_send[...] = total.astype(jnp.bfloat16).reshape(rows_send.shape)
    sent += dispatch(rows_send, rows_all, rows_sems, rows_wall_sems)
    for b in range(2):
        new_ref.reshape(flat, 128)[pl.ds(b, POINTS, stride=2)] = new[:POINTS, b * 128 : (b + 1) * 128]
    sent += pass_on(rows_all, rows_sems, rows_wall_sems)
    for copy, sends, _ in halos:
        pl.when(sends)(copy.wait_send)
    for copy in sent:
        copy.wait_send()
    finish(marks_all, marks_wall_sems)
    finish(rows_all, rows_wall_sems)


def train_kernel(
    per_chunk, full,
    new_ref, rows_all, marks_all, one, two, three, four, five,
    new_out, out_one, out_two, out_three, out_four, out_five,
    grad_one, grad_two, grad_three, grad_four, grad_five, sems,
):
    copies = [pltpu.make_async_copy(new_ref, new_out, sems.at[5])]
    copies[0].start()
    walls, spans = rows_all.shape[:2]
    weights = (one, two, three, four, five)
    grads = (grad_one, grad_two, grad_three, grad_four, grad_five)
    outs = (out_one, out_two, out_three, out_four, out_five)
    chunks = walls // per_chunk
    places = spans * CAP
    count = per_chunk * places

    def leave(layer):
        copy = pltpu.make_async_copy(grads[layer], outs[layer], sems.at[layer])
        copy.start()
        copies.append(copy)

    def chunk(number):
        first = number * per_chunk
        act = rows_all[pl.ds(first, per_chunk)].reshape(count, -1)
        picked = marks_all.at[pl.ds(first, per_chunk)]
        wanted = picked[:, :, 0:CAP].reshape(count, -1).astype(jnp.float32)
        if full:
            scale = np.float32(1.0 / places)
        else:
            flags = picked[:, :, CAP : 2 * CAP].reshape(per_chunk, places, -1).astype(jnp.float32)
            scale = flags / jnp.maximum(jnp.sum(flags, axis=1, keepdims=True), 1.0)
            scale = scale.reshape(count, -1)
        acts = [act]
        slopes = []
        for layer in weights[:-1]:
            pre = jnp.dot(act, layer[0], preferred_element_type=jnp.float32)
            sigma = 0.5 + 0.5 * jnp.tanh(0.5 * pre)
            hidden = pre * sigma
            slopes.append(sigma + hidden * (1.0 - sigma))
            act = hidden.astype(jnp.bfloat16)
            acts.append(act)
        output = jnp.dot(act, weights[-1][0], preferred_element_type=jnp.float32)
        error = (scale * (output - wanted)).astype(jnp.bfloat16)
        for layer in range(4, -1, -1):
            grad = lax.dot_general(
                acts[layer], error, (((0,), (0,)), ((), ())), preferred_element_type=jnp.float32
            )
            if chunks == 1:
                grads[layer][0] = grad
                leave(layer)
            else:
                grads[layer][0] += grad
            if layer:
                back = lax.dot_general(
                    error, weights[layer][0], (((1,), (1,)), ((), ())), preferred_element_type=jnp.float32
                )
                error = (back * slopes[layer - 1]).astype(jnp.bfloat16)

    if chunks == 1:
        chunk(0)
    else:
        for grad in grads:
            grad[...] = jnp.zeros_like(grad)
        pl.loop(0, chunks)(chunk)
        for layer in range(5):
            leave(layer)
    for copy in copies:
        copy.wait()


def local(spans, walls, field, velocity, cells, destination, targets, *weights):
    shape = field.shape
    samples = cells.shape[0]
    inside = (P_SIZE, P_SIZE, P_SIZE, shape[3] * shape[4], shape[5])
    vmem = pl.BlockSpec(memory_space=pltpu.VMEM)
    anywhere = pl.BlockSpec(memory_space=pl.ANY)
    hbm = pl.BlockSpec(memory_space=pltpu.HBM)
    features = P_SIZE**3 + 3
    wide = targets.shape[1]
    full = is_full(spans, samples)
    marks = CAP if full else 2 * CAP
    dma = pltpu.SemaphoreType.DMA
    new_field, *received = pl.pallas_call(
        functools.partial(section_kernel, spans, walls),
        out_shape=(
            jax.ShapeDtypeStruct(inside, jnp.float32),
            jax.ShapeDtypeStruct((walls, spans, CAP, features), jnp.bfloat16),
            jax.ShapeDtypeStruct((walls, spans, marks, wide), jnp.bfloat16),
        ),
        in_specs=[hbm] * 7,
        out_specs=(vmem,) * 3,
        scratch_shapes=[
            pltpu.VMEM((256, 128), jnp.float32),
            pltpu.VMEM((3, 256, 128), jnp.float32),
            pltpu.VMEM((1, samples), jnp.int32),
            pltpu.VMEM((1, samples), jnp.int32),
            pltpu.VMEM(targets.shape, jnp.bfloat16),
            pltpu.VMEM(FACE_TABLE.shape, jnp.bfloat16),
            pltpu.VMEM(POINT_TABLE.shape, jnp.bfloat16),
            pltpu.VMEM((2, 2, FACES, 256), jnp.bfloat16),
            pltpu.VMEM((2, 2, FACES, 128), jnp.bfloat16),
            pltpu.VMEM((2, FACES, 256), jnp.bfloat16),
            pltpu.VMEM((2, FACES, 256), jnp.bfloat16),
            pltpu.VMEM((2, FACES, 128), jnp.bfloat16),
            pltpu.VMEM((2, FACES, 128), jnp.bfloat16),
            pltpu.VMEM((128, 256), jnp.float32),
            pltpu.VMEM((spans, CAP, features), jnp.bfloat16),
            pltpu.VMEM((spans, marks, wide), jnp.bfloat16),
            dma((9,)), dma((4,)), dma((4,)),
            dma((2, spans)), dma((2, walls, min(spans, COPIES))), dma((2, spans)), dma((2, walls, min(spans, COPIES))),
        ],
        compiler_params=pltpu.CompilerParams(
            collective_id=0, has_side_effects=True, vmem_limit_bytes=48 * 1024 * 1024
        ),
        name="section",
    )(
        *(
            pltpu.with_memory_space_constraint(x, pltpu.HBM)
            for x in (
                field.reshape(inside),
                velocity.reshape((3,) + inside),
                cells.reshape(1, samples),
                destination.reshape(1, samples),
                targets,
                jnp.asarray(FACE_TABLE),
                jnp.asarray(POINT_TABLE),
            )
        )
    )
    per_chunk = max(1, min(walls, 512 // (spans * CAP)))
    while walls % per_chunk:
        per_chunk -= 1
    outs = pl.pallas_call(
        functools.partial(train_kernel, per_chunk, full),
        out_shape=(jax.ShapeDtypeStruct(inside, jnp.float32),)
        + tuple(jax.ShapeDtypeStruct(x.shape, jnp.float32) for x in weights),
        in_specs=[anywhere] + [vmem] * 7,
        out_specs=(anywhere,) * 6,
        scratch_shapes=[pltpu.VMEM(x.shape, jnp.float32) for x in weights] + [dma((6,))],
        compiler_params=pltpu.CompilerParams(vmem_limit_bytes=48 * 1024 * 1024),
        name="train",
    )(new_field, *received, *weights)
    return (outs[0].reshape(shape),) + tuple(outs[1:])


def solution(mesh):
    in_specs = (
        P(None, None, None, "span", "wall", None),
        P(None, None, None, None, "span", "wall", None),
        P(("span", "wall")),
        P(("span", "wall"), None),
        P(("span", "wall"), None),
        P("span", None, None),
        P("span", None, None),
        P("span", None, None),
        P("span", None, None),
        P("span", None, None),
    )
    out_specs = (
        P(None, None, None, "span", "wall", None),
        P("span", None, None),
        P("span", None, None),
        P("span", None, None),
        P("span", None, None),
        P("span", None, None),
    )
    body = functools.partial(local, mesh.shape["span"], mesh.shape["wall"])
    return jax.shard_map(body, mesh=mesh, in_specs=in_specs, out_specs=out_specs, check_vma=False)
```

```python
import functools
import math

import jax
import jax.numpy as jnp
import numpy as np
from jax import lax
from jax.experimental import pallas as pl
from jax.experimental.pallas import tpu as pltpu
from jax.sharding import PartitionSpec as P

P_SIZE = 5
CAP = 16
COPIES = 1
MESH = pl.DeviceIdType.MESH


step_scale = 0.04


def legendre_pair(order, point):
    value_prev = 1.0
    value_now = point
    slope_prev = 0.0
    slope_now = 1.0
    for degree in range(1, order):
        value_next = ((2 * degree + 1) * point * value_now - degree * value_prev) / (degree + 1)
        slope_next = slope_prev + (2 * degree + 1) * value_now
        value_prev, value_now = (value_now, value_next)
        slope_prev, slope_now = (slope_now, slope_next)
    return (value_now, slope_now)


def gauss_nodes(count):
    found = []
    for index in range(count):
        guess = math.cos(math.pi * (index + 0.75) / (count + 0.5))
        for sweep in range(60):
            value, slope = legendre_pair(count, guess)
            guess = guess - value / slope
        found.append(guess)
    return sorted(found)


def fr_tables():
    nodes = gauss_nodes(P_SIZE)
    bary = []
    for j in range(P_SIZE):
        product = 1.0
        for m in range(P_SIZE):
            if m != j:
                product = product * (nodes[j] - nodes[m])
        bary.append(1.0 / product)
    deriv = [[0.0] * P_SIZE for row_index in range(P_SIZE)]
    for i in range(P_SIZE):
        for j in range(P_SIZE):
            if i != j:
                deriv[i][j] = bary[j] / bary[i] / (nodes[i] - nodes[j])
        deriv[i][i] = -sum((deriv[i][j] for j in range(P_SIZE) if j != i))

    def basis_at(point):
        values = []
        for j in range(P_SIZE):
            product = 1.0
            for m in range(P_SIZE):
                if m != j:
                    product = product * (point - nodes[m]) / (nodes[j] - nodes[m])
            values.append(product)
        return values

    left_value = basis_at(-1.0)
    right_value = basis_at(1.0)
    sign = (-1.0) ** P_SIZE
    slope_left = [
        0.5 * sign * (legendre_pair(P_SIZE, x)[1] - legendre_pair(P_SIZE - 1, x)[1]) for x in nodes
    ]
    slope_right = [-slope_left[P_SIZE - 1 - i] for i in range(P_SIZE)]
    inner = [
        [
            step_scale
            * (deriv[i][m] - slope_left[i] * left_value[m] - slope_right[i] * right_value[m])
            for m in range(P_SIZE)
        ]
        for i in range(P_SIZE)
    ]
    edge_left = [0.25 * step_scale * s for s in slope_left]
    edge_right = [0.25 * step_scale * s for s in slope_right]
    return inner, left_value, right_value, edge_left, edge_right


POINTS = P_SIZE**3
FACES = 32


def section_tables():
    inner, left, right, edge_left, edge_right = fr_tables()
    to_faces = np.zeros((3, 2, FACES, 128))
    volume = np.zeros((128, 3, 128))
    edges = np.zeros((128, 3, 2, FACES))
    for point in range(POINTS):
        place = (point // 25, point // 5 % 5, point % 5)
        for d in range(3):
            rest = [place[n] for n in range(3) if n != d]
            face = rest[0] * P_SIZE + rest[1]
            to_faces[d, 0, face, point] = left[place[d]]
            to_faces[d, 1, face, point] = right[place[d]]
            edges[point, d, 0, face] = edge_left[place[d]]
            edges[point, d, 1, face] = edge_right[place[d]]
            for m in range(P_SIZE):
                source = point + (m - place[d]) * (25, 5, 1)[d]
                volume[point, d, source] = inner[place[d]][m]

    def halves(table):
        high = table.astype(np.float32).astype(jnp.bfloat16)
        low = (table - high.astype(np.float64)).astype(np.float32).astype(jnp.bfloat16)
        return np.stack([high, low])

    second = np.concatenate([volume.reshape(128, -1), edges.reshape(128, -1)], axis=1)
    return halves(to_faces.reshape(-1, 128)), halves(second)


FACE_TABLE, POINT_TABLE = section_tables()


def apply(table, x):
    high = x.astype(jnp.bfloat16)
    low = (x - high.astype(jnp.float32)).astype(jnp.bfloat16)
    return jnp.dot(
        jnp.concatenate([table[0], table[0], table[1]], axis=1),
        jnp.concatenate([high, low, high], axis=0),
        preferred_element_type=jnp.float32,
    )


def upwind(state_before, speed_before, state_after, speed_after):
    speed = speed_before + speed_after
    return speed * (state_before + state_after) - jnp.abs(speed) * (state_after - state_before)


def turn(x, step):
    half = x.shape[1] // 2
    return jnp.concatenate([pltpu.roll(x[:, :half], step % half, 1), pltpu.roll(x[:, half:], step % half, 1)], axis=1)


def paired(place, d):
    bit = 1
    while bit <= d:
        if d & bit:
            place = place + bit * (1 - 2 * lax.rem(lax.div(place, bit), 2))
        bit *= 2
    return place


def is_full(spans, samples):
    return spans * CAP == samples


def section_kernel(
    spans, walls,
    field_hbm, velocity_hbm, cells_hbm, dest_hbm, targets_hbm, face_hbm, point_hbm,
    new_ref, rows_all, marks_all,
    field, velocity, cells_ref, dest_ref, targets_ref, face_table, point_table,
    zero_send, one_send, zero_before, zero_after, one_before, one_after,
    rows_send, marks_send,
    in_sems, halo_send, halo_recv,
    marks_sems, marks_wall_sems, rows_sems, rows_wall_sems,
):
    i = lax.axis_index("span")
    w = lax.axis_index("wall")
    barrier = pltpu.get_barrier_semaphore()
    for d in reversed(range(1, spans)):
        pl.semaphore_signal(barrier, inc=1, device_id={"span": paired(i, d)}, device_id_type=MESH)
    for d in reversed(range(1, walls)):
        pl.semaphore_signal(barrier, inc=1, device_id={"wall": paired(w, d)}, device_id_type=MESH)

    flat = 2 * POINTS
    loads = [
        pltpu.make_async_copy(field_hbm.reshape(flat, 128), field.at[0:flat], in_sems.at[0]),
        pltpu.make_async_copy(face_hbm, face_table, in_sems.at[1]),
    ]
    for d in range(3):
        loads.append(
            pltpu.make_async_copy(velocity_hbm.at[d].reshape(flat, 128), velocity.at[d, 0:flat], in_sems.at[2 + d])
        )
    for number, (whole, ref) in enumerate(
        ((dest_hbm, dest_ref), (targets_hbm, targets_ref), (cells_hbm, cells_ref), (point_hbm, point_table))
    ):
        loads.append(pltpu.make_async_copy(whole, ref, in_sems.at[5 + number]))
    for load in loads:
        load.start()

    for at_end, ref in ((i == 0, zero_before), (i == spans - 1, zero_after), (w == 0, one_before), (w == walls - 1, one_after)):
        @pl.when(at_end)
        def _(ref=ref):
            ref[...] = jnp.zeros_like(ref)

    field[flat:] = jnp.zeros((256 - flat, 128), jnp.float32)
    velocity[:, flat:] = jnp.zeros((3, 256 - flat, 128), jnp.float32)

    def beside(ref, *at):
        return jnp.concatenate([ref[at + (pl.ds(b, 128, stride=2),)] for b in range(2)], axis=1)

    loads[0].wait()
    loads[1].wait()
    two = 2 * FACES
    q = beside(field)
    face_q = apply(face_table[:, 0 : 2 * two], q)
    q_zero, q_one = face_q[:two], face_q[two:]
    loads[2].wait()
    a_zero = apply(face_table[:, 0:two], beside(velocity, 0))
    loads[3].wait()
    a_one = apply(face_table[:, two : 2 * two], beside(velocity, 1))
    for n, (along_zero, along_one) in enumerate(((q_zero, q_one), (a_zero, a_one))):
        zero_send[0, n] = along_zero[:FACES]
        zero_send[1, n] = along_zero[FACES:]
        one_send[0, n] = along_one[:FACES, :128]
        one_send[1, n] = along_one[FACES:, 128:]

    pl.semaphore_wait(barrier, spans + walls - 2)

    def halo(number, axis, place, count, source, into, right):
        peer = jnp.minimum(place + 1, count - 1) if right else jnp.maximum(place - 1, 0)
        copy = pltpu.make_async_remote_copy(
            src_ref=source,
            dst_ref=into,
            send_sem=halo_send.at[number],
            recv_sem=halo_recv.at[number],
            device_id={axis: peer},
            device_id_type=MESH,
        )
        sends = place < count - 1 if right else place > 0
        gets = place > 0 if right else place < count - 1
        return copy, sends, gets

    halos = [
        halo(2, "wall", w, walls, one_send.at[1], one_before, True),
        halo(3, "wall", w, walls, one_send.at[0], one_after, False),
        halo(0, "span", i, spans, zero_send.at[1], zero_before, True),
        halo(1, "span", i, spans, zero_send.at[0], zero_after, False),
    ]
    for copy, sends, _ in halos:
        pl.when(sends)(copy.start)

    samples = dest_ref.shape[1]
    for load in loads[5:8]:
        load.wait()
    dest = dest_ref[...]
    across = jnp.broadcast_to(dest, (samples, samples))
    down = jnp.transpose(across)
    earlier = lax.broadcasted_iota(jnp.int32, (samples, samples), 0) < lax.broadcasted_iota(jnp.int32, (samples, samples), 1)
    slot = jnp.sum(jnp.where(jnp.logical_and(across == down, earlier), 1.0, 0.0), axis=0, keepdims=True)
    position = dest * CAP + slot.astype(jnp.int32)
    places = spans * CAP
    chosen = jnp.where(
        lax.broadcasted_iota(jnp.int32, (places, samples), 0) == position, 1.0, 0.0
    ).astype(jnp.bfloat16)
    wanted = jnp.dot(chosen, targets_ref[...], preferred_element_type=jnp.float32)
    marks_send[:, 0:CAP] = wanted.astype(jnp.bfloat16).reshape(spans, CAP, -1)
    if not is_full(spans, samples):
        flags = jnp.dot(chosen, jnp.ones((samples, samples), jnp.bfloat16), preferred_element_type=jnp.float32)
        marks_send[:, CAP : 2 * CAP] = flags.astype(jnp.bfloat16).reshape(spans, CAP, -1)

    groups = min(spans, COPIES)
    size = spans // groups

    def group_of(held, wall, g):
        return held.at[wall, pl.ds(paired(lax.div(i, size), g) * size, size)]

    def dispatch(send, held, sems, wall_sems):
        copies = [
            pltpu.make_async_remote_copy(
                src_ref=send.at[paired(i, d)],
                dst_ref=held.at[w, i],
                send_sem=sems.at[0, d],
                recv_sem=sems.at[1, d],
                device_id={"span": paired(i, d)},
                device_id_type=MESH,
            )
            for d in reversed(range(1, spans))
        ]
        for copy in copies:
            copy.start()
        held[w, i] = send[i]
        if size == 1:
            copies = copies + forward(held, wall_sems, 0)
        return copies

    def forward(held, sems, g):
        place = group_of(held, w, g)
        copies = [
            pltpu.make_async_remote_copy(
                src_ref=place,
                dst_ref=place,
                send_sem=sems.at[0, n, g],
                recv_sem=sems.at[1, n, g],
                device_id={"wall": paired(w, n)},
                device_id_type=MESH,
            )
            for n in reversed(range(1, walls))
        ]
        for copy in copies:
            copy.start()
        return copies

    def pass_on(held, sems, wall_sems):
        copies = []
        for d in range(1, spans):
            source = paired(i, d)
            pltpu.make_async_remote_copy(
                src_ref=held.at[w, source],
                dst_ref=held.at[w, source],
                send_sem=sems.at[0, d],
                recv_sem=sems.at[1, d],
                device_id={"span": source},
                device_id_type=MESH,
            ).wait_recv()
            if (d + 1) % size == 0:
                copies += forward(held, wall_sems, d // size)
        return copies

    def finish(held, sems):
        for g in range(groups):
            for n in range(1, walls):
                place = group_of(held, paired(w, n), g)
                pltpu.make_async_remote_copy(
                    src_ref=place,
                    dst_ref=place,
                    send_sem=sems.at[0, n, g],
                    recv_sem=sems.at[1, n, g],
                    device_id={"wall": paired(w, n)},
                    device_id_type=MESH,
                ).wait_recv()

    sent = dispatch(marks_send, marks_all, marks_sems, marks_wall_sems)

    cells = cells_ref[...]
    here = jnp.where(
        lax.broadcasted_iota(jnp.int32, (2 * samples, samples), 0) == cells, 1.0, 0.0
    ).astype(jnp.bfloat16)
    picks = lax.dot_general(
        chosen, here, (((1,), (1,)), ((), ())), preferred_element_type=jnp.float32
    ).astype(jnp.bfloat16)

    loads[4].wait()
    loads[8].wait()
    a = [beside(velocity, d) for d in range(3)]
    q_two = apply(face_table[:, 2 * two :], q)
    a_two = apply(face_table[:, 2 * two :], a[2])
    left = upwind(turn(q_two[FACES:], 1), turn(a_two[FACES:], 1), q_two[:FACES], a_two[:FACES])
    right = upwind(q_two[FACES:], a_two[FACES:], turn(q_two[:FACES], -1), turn(a_two[:FACES], -1))
    edges = 3 * 128
    partial = q - (
        apply(point_table[:, :, :edges], jnp.concatenate([q * x for x in a], axis=0))
        + apply(point_table[:, :, edges + 2 * two :], jnp.concatenate([left, right], axis=0))
    )
    row = lax.broadcasted_iota(jnp.int32, partial.shape, 0)
    for d in range(3):
        mean = jnp.sum(a[d], axis=0, keepdims=True) * np.float32(1.0 / POINTS)
        partial = jnp.where(row == POINTS + d, mean, partial)


    for copy, _, gets in halos:
        pl.when(gets)(copy.wait_recv)
    got = [[ref[n] for n in range(2)] for ref in (zero_before, zero_after, one_before, one_after)]
    shared = [
        upwind(*got[0], q_zero[:FACES], a_zero[:FACES]),
        upwind(q_zero[FACES:], a_zero[FACES:], *got[1]),
    ]
    before = [jnp.concatenate([got[2][n], x[FACES:, :128]], axis=1) for n, x in enumerate((q_one, a_one))]
    after = [jnp.concatenate([x[:FACES, 128:], got[3][n]], axis=1) for n, x in enumerate((q_one, a_one))]
    shared.append(upwind(before[0], before[1], q_one[:FACES], a_one[:FACES]))
    shared.append(upwind(q_one[FACES:], a_one[FACES:], after[0], after[1]))
    new = partial - apply(point_table[:, :, edges : edges + 2 * two], jnp.concatenate(shared, axis=0))
    total = lax.dot_general(
        picks, new.astype(jnp.bfloat16), (((1,), (1,)), ((), ())), preferred_element_type=jnp.float32
    )
    rows_send[...] = total.astype(jnp.bfloat16).reshape(rows_send.shape)
    sent += dispatch(rows_send, rows_all, rows_sems, rows_wall_sems)
    sent += pass_on(marks_all, marks_sems, marks_wall_sems)
    for b in range(2):
        new_ref.reshape(flat, 128)[pl.ds(b, POINTS, stride=2)] = new[:POINTS, b * 128 : (b + 1) * 128]
    sent += pass_on(rows_all, rows_sems, rows_wall_sems)
    for copy, sends, _ in halos:
        pl.when(sends)(copy.wait_send)
    for copy in sent:
        copy.wait_send()
    finish(marks_all, marks_wall_sems)
    finish(rows_all, rows_wall_sems)


def train_kernel(
    per_chunk, full,
    new_ref, rows_all, marks_all, one, two, three, four, five,
    new_out, out_one, out_two, out_three, out_four, out_five,
    grad_one, grad_two, grad_three, grad_four, grad_five, sems,
):
    copies = [pltpu.make_async_copy(new_ref, new_out, sems.at[5])]
    copies[0].start()
    walls, spans = rows_all.shape[:2]
    weights = (one, two, three, four, five)
    grads = (grad_one, grad_two, grad_three, grad_four, grad_five)
    outs = (out_one, out_two, out_three, out_four, out_five)
    chunks = walls // per_chunk
    places = spans * CAP
    count = per_chunk * places

    def leave(layer):
        copy = pltpu.make_async_copy(grads[layer], outs[layer], sems.at[layer])
        copy.start()
        copies.append(copy)

    def chunk(number):
        first = number * per_chunk
        act = rows_all[pl.ds(first, per_chunk)].reshape(count, -1)
        picked = marks_all.at[pl.ds(first, per_chunk)]
        wanted = picked[:, :, 0:CAP].reshape(count, -1).astype(jnp.float32)
        if full:
            scale = np.float32(1.0 / places)
        else:
            flags = picked[:, :, CAP : 2 * CAP].reshape(per_chunk, places, -1).astype(jnp.float32)
            scale = flags / jnp.maximum(jnp.sum(flags, axis=1, keepdims=True), 1.0)
            scale = scale.reshape(count, -1)
        acts = [act]
        slopes = []
        for layer in weights[:-1]:
            pre = jnp.dot(act, layer[0], preferred_element_type=jnp.float32)
            sigma = 0.5 + 0.5 * jnp.tanh(0.5 * pre)
            hidden = pre * sigma
            slopes.append(sigma + hidden * (1.0 - sigma))
            act = hidden.astype(jnp.bfloat16)
            acts.append(act)
        output = jnp.dot(act, weights[-1][0], preferred_element_type=jnp.float32)
        error = (scale * (output - wanted)).astype(jnp.bfloat16)
        for layer in range(4, -1, -1):
            grad = lax.dot_general(
                acts[layer], error, (((0,), (0,)), ((), ())), preferred_element_type=jnp.float32
            )
            if chunks == 1:
                grads[layer][0] = grad
                leave(layer)
            else:
                grads[layer][0] += grad
            if layer:
                back = lax.dot_general(
                    error, weights[layer][0], (((1,), (1,)), ((), ())), preferred_element_type=jnp.float32
                )
                error = (back * slopes[layer - 1]).astype(jnp.bfloat16)

    if chunks == 1:
        chunk(0)
    else:
        for grad in grads:
            grad[...] = jnp.zeros_like(grad)
        pl.loop(0, chunks)(chunk)
        for layer in range(5):
            leave(layer)
    for copy in copies:
        copy.wait()


def local(spans, walls, field, velocity, cells, destination, targets, *weights):
    shape = field.shape
    samples = cells.shape[0]
    inside = (P_SIZE, P_SIZE, P_SIZE, shape[3] * shape[4], shape[5])
    vmem = pl.BlockSpec(memory_space=pltpu.VMEM)
    anywhere = pl.BlockSpec(memory_space=pl.ANY)
    hbm = pl.BlockSpec(memory_space=pltpu.HBM)
    features = P_SIZE**3 + 3
    wide = targets.shape[1]
    full = is_full(spans, samples)
    marks = CAP if full else 2 * CAP
    dma = pltpu.SemaphoreType.DMA
    new_field, *received = pl.pallas_call(
        functools.partial(section_kernel, spans, walls),
        out_shape=(
            jax.ShapeDtypeStruct(inside, jnp.float32),
            jax.ShapeDtypeStruct((walls, spans, CAP, features), jnp.bfloat16),
            jax.ShapeDtypeStruct((walls, spans, marks, wide), jnp.bfloat16),
        ),
        in_specs=[hbm] * 7,
        out_specs=(vmem,) * 3,
        scratch_shapes=[
            pltpu.VMEM((256, 128), jnp.float32),
            pltpu.VMEM((3, 256, 128), jnp.float32),
            pltpu.VMEM((1, samples), jnp.int32),
            pltpu.VMEM((1, samples), jnp.int32),
            pltpu.VMEM(targets.shape, jnp.bfloat16),
            pltpu.VMEM(FACE_TABLE.shape, jnp.bfloat16),
            pltpu.VMEM(POINT_TABLE.shape, jnp.bfloat16),
            pltpu.VMEM((2, 2, FACES, 256), jnp.float32),
            pltpu.VMEM((2, 2, FACES, 128), jnp.float32),
            pltpu.VMEM((2, FACES, 256), jnp.float32),
            pltpu.VMEM((2, FACES, 256), jnp.float32),
            pltpu.VMEM((2, FACES, 128), jnp.float32),
            pltpu.VMEM((2, FACES, 128), jnp.float32),
            pltpu.VMEM((spans, CAP, features), jnp.bfloat16),
            pltpu.VMEM((spans, marks, wide), jnp.bfloat16),
            dma((9,)), dma((4,)), dma((4,)),
            dma((2, spans)), dma((2, walls, min(spans, COPIES))), dma((2, spans)), dma((2, walls, min(spans, COPIES))),
        ],
        compiler_params=pltpu.CompilerParams(
            collective_id=0, has_side_effects=True, vmem_limit_bytes=48 * 1024 * 1024
        ),
        name="section",
    )(
        *(
            pltpu.with_memory_space_constraint(x, pltpu.HBM)
            for x in (
                field.reshape(inside),
                velocity.reshape((3,) + inside),
                cells.reshape(1, samples),
                destination.reshape(1, samples),
                targets,
                jnp.asarray(FACE_TABLE),
                jnp.asarray(POINT_TABLE),
            )
        )
    )
    per_chunk = max(1, min(walls, 512 // (spans * CAP)))
    while walls % per_chunk:
        per_chunk -= 1
    outs = pl.pallas_call(
        functools.partial(train_kernel, per_chunk, full),
        out_shape=(jax.ShapeDtypeStruct(inside, jnp.float32),)
        + tuple(jax.ShapeDtypeStruct(x.shape, jnp.float32) for x in weights),
        in_specs=[anywhere] + [vmem] * 7,
        out_specs=(anywhere,) * 6,
        scratch_shapes=[pltpu.VMEM(x.shape, jnp.float32) for x in weights] + [dma((6,))],
        compiler_params=pltpu.CompilerParams(vmem_limit_bytes=48 * 1024 * 1024),
        name="train",
    )(new_field, *received, *weights)
    return (outs[0].reshape(shape),) + tuple(outs[1:])


def solution(mesh):
    in_specs = (
        P(None, None, None, "span", "wall", None),
        P(None, None, None, None, "span", "wall", None),
        P(("span", "wall")),
        P(("span", "wall"), None),
        P(("span", "wall"), None),
        P("span", None, None),
        P("span", None, None),
        P("span", None, None),
        P("span", None, None),
        P("span", None, None),
    )
    out_specs = (
        P(None, None, None, "span", "wall", None),
        P("span", None, None),
        P("span", None, None),
        P("span", None, None),
        P("span", None, None),
        P("span", None, None),
    )
    body = functools.partial(local, mesh.shape["span"], mesh.shape["wall"])
    return jax.shard_map(body, mesh=mesh, in_specs=in_specs, out_specs=out_specs, check_vma=False)
```
